128 devices in a mesh: dp: 32 (over x, z_lo, y), ctx: 4 (over z_hi, core).
Axes of the slice: x: 4, y: 4, z: 4 (z_hi: 2, z_lo: 2; z = z_hi * 2 + z_lo), core: 2. Of those that a mesh axis runs over, the one named last changes fastest.
Arguments:
- tokens: bfloat16 [32, 2048, 576], P('dp', 'ctx'), may hold values from -6 to 6
- cotangent: bfloat16 [32, 2048, 576], P('dp', 'ctx'), may hold values from -6 to 6
- gain_attn: bfloat16 [576], P('dp'), may hold values from 0.099609375 to 1.8984375
- gain_mlp: bfloat16 [576], P('dp'), may hold values from 0.099609375 to 1.8984375
- w_query: bfloat16 [576, 576], P('dp', 'ctx'), may hold values from -0.25 to 0.25
- w_key: bfloat16 [576, 192], P('dp', 'ctx'), may hold values from -0.25 to 0.25
- w_value: bfloat16 [576, 192], P('dp', 'ctx'), may hold values from -0.25 to 0.25
- w_out: bfloat16 [576, 576], P('dp', 'ctx'), may hold values from -3 to 3
- w_gate: bfloat16 [576, 1536], P('dp', 'ctx'), may hold values from -0.25 to 0.25
- w_up: bfloat16 [576, 1536], P('dp', 'ctx'), may hold values from -0.25 to 0.25
- w_down: bfloat16 [1536, 576], P('dp', 'ctx'), may hold values from -0.15625 to 0.15625
Outputs:
- output: bfloat16 [32, 2048, 576], P('dp', 'ctx')
- grad_tokens: float32 [32, 2048, 576], P('dp', 'ctx')
- grad_gain_attn: float32 [576], P('dp')
- grad_gain_mlp: float32 [576], P('dp')
- grad_query: float32 [576, 576], P('dp', 'ctx')
- grad_key: float32 [576, 192], P('dp', 'ctx')
- grad_value: float32 [576, 192], P('dp', 'ctx')
- grad_out: float32 [576, 576], P('dp', 'ctx')
- grad_gate: float32 [576, 1536], P('dp', 'ctx')
- grad_up: float32 [576, 1536], P('dp', 'ctx')
- grad_down: float32 [1536, 576], P('dp', 'ctx')
The draws below stay inside these ranges and needn't reach their ends.
All inputs are finite; a program needn't handle non-finite values.
Results may differ from the reference program's by a relative error of at most 0.013.
Values may be sent and summed in bfloat16 or wider, within the bound.
A program may use at most 256 MiB of HBM per device.

```python
import jax
import jax.numpy as jnp
from jax import lax

D = 576
HEADS = 9
KV_HEADS = 3
HEAD = 64
FF = 1536
LENGTH = 2048
SEQS = 32
N_CTX = 4


def shard_levels(stream_key, dims, cuts, least, largest):
    factor_of, own = 1.0, jax.random.fold_in(stream_key, 6)
    for dim, blocks in cuts:
        draws = jnp.exp(jax.random.uniform(jax.random.fold_in(own, dim), (blocks,), jnp.float32, least / len(cuts), largest / len(cuts)))
        factor_of = factor_of * jnp.repeat(draws, dims[dim] // blocks).reshape([-1 if axis == dim else 1 for axis in range(len(dims))])
    return factor_of


def gaussian(rng, extent, scale, limit, pieces=(), kind=jnp.bfloat16):
    array = scale * jax.random.normal(rng, extent, jnp.float32)
    if pieces:
        array = array * shard_levels(rng, extent, pieces, -0.22, 0.18)
    return jnp.clip(array, -limit, limit).astype(kind)


def setup_inputs(seed: int = 0) -> dict:
    key_list = jax.random.split(jax.random.key(seed), 12)
    tokens = gaussian(key_list[0], (SEQS, LENGTH, D), 1.0, 6.0, ((0, 32), (1, 4)))
    cotangent = gaussian(key_list[1], (SEQS, LENGTH, D), 1.0, 6.0, ((0, 32), (1, 4)))
    gain_attn = jnp.clip(1.0 + 0.18 * jax.random.normal(key_list[2], (D,), jnp.float32), 0.099609375, 1.8984375).astype(jnp.bfloat16)
    gain_mlp = jnp.clip(1.0 + 0.18 * jax.random.normal(key_list[3], (D,), jnp.float32), 0.099609375, 1.8984375).astype(jnp.bfloat16)
    w_query = gaussian(key_list[4], (D, HEADS * HEAD), D ** -0.5, 0.25, ((0, 32), (1, 4)))
    w_key = gaussian(key_list[5], (D, KV_HEADS * HEAD), D ** -0.5, 0.25, ((0, 32), (1, 4)))
    w_value = gaussian(key_list[6], (D, KV_HEADS * HEAD), D ** -0.5, 0.25, ((0, 32), (1, 4)))
    w_out = gaussian(key_list[7], (HEADS * HEAD, D), (max(D // 128, 1)) ** -0.5, 3.0, ((0, 32), (1, 4)))
    w_gate = gaussian(key_list[8], (D, FF), D ** -0.5, 0.25, ((0, 32), (1, 4)))
    w_up = gaussian(key_list[9], (D, FF), D ** -0.5, 0.25, ((0, 32), (1, 4)))
    w_down = gaussian(key_list[10], (FF, D), FF ** -0.5, 0.15625, ((0, 32), (1, 4)))
    return dict(tokens=tokens, cotangent=cotangent, gain_attn=gain_attn, gain_mlp=gain_mlp, w_query=w_query, w_key=w_key, w_value=w_value, w_out=w_out, w_gate=w_gate, w_up=w_up, w_down=w_down)


@jax.custom_vjp
def low(v):
    return lax.optimization_barrier(v.astype(jnp.bfloat16)).astype(jnp.float32)

@jax.custom_vjp
def low_back(v):
    return v

def low_keep(v):
    return (low(v), None)

def low_pass(kept, grad):
    return (grad,)

def back_keep(v):
    return (v, None)

def back_low(kept, grad):
    return (low(grad),)
low.defvjp(low_keep, low_pass)
low_back.defvjp(back_keep, back_low)

def positions(count):
    rows = count // N_CTX
    half = rows // 2
    index = jnp.arange(count, dtype=jnp.int32)
    device = index // rows
    within = index % rows
    block = jnp.where(within < half, device, 2 * N_CTX - 1 - device)
    return (block * half + within % half).astype(jnp.int32)

def angles(pos, size):
    half = size // 2
    freq = 100000.0 ** (-jnp.arange(half, dtype=jnp.float32) * 2.0 / size)
    angle = pos.astype(jnp.float32)[:, None] * freq[None, :]
    return (jnp.cos(angle)[:, None, :], jnp.sin(angle)[:, None, :])

def rotate(vector, pos):
    half = vector.shape[-1] // 2
    cosine, sine = angles(pos, vector.shape[-1])
    first = vector[..., :half]
    second = vector[..., half:]
    return jnp.concatenate([first * cosine - second * sine, second * cosine + first * sine], -1)

def layer(inputs, gain_one, gain_two, wq, wk, wv, wo, wg, wu, wd):
    high = lax.Precision.HIGHEST
    length = inputs.shape[0]
    groups = HEADS // KV_HEADS
    pos = positions(length)
    scale_one = lax.rsqrt(lax.optimization_barrier(jnp.mean(inputs * inputs, -1, keepdims=True)) + 1e-05)
    normed = low(inputs * scale_one * gain_one)
    query_pre = low_back(jnp.dot(normed, wq, precision=high))
    key_pre = low_back(jnp.dot(normed, wk, precision=high))
    values = low(low_back(jnp.dot(normed, wv, precision=high))).reshape(length, KV_HEADS, HEAD)
    query = low(rotate(query_pre.reshape(length, HEADS, HEAD), pos)).reshape(length, KV_HEADS, groups, HEAD)
    keys = low(rotate(key_pre.reshape(length, KV_HEADS, HEAD), pos))
    scores = jnp.einsum('qkgd,jkd->kgqj', query, keys, precision=high) * HEAD ** (-0.5)
    scores = low_back(scores)
    allowed = pos[:, None] >= pos[None, :]
    scores = jnp.where(allowed, scores, -1e+30)
    probs = low(jax.nn.softmax(scores, axis=-1))
    mixed = jnp.einsum('kgqj,jkd->qkgd', probs, values, precision=high).reshape(length, HEADS * HEAD)
    mixed = low_back(low(mixed))
    middle = inputs + low_back(jnp.dot(mixed, wo, precision=high))
    scale_two = lax.rsqrt(lax.optimization_barrier(jnp.mean(middle * middle, -1, keepdims=True)) + 1e-05)
    normed_two = low(middle * scale_two * gain_two)
    gate = low_back(jnp.dot(normed_two, wg, precision=high))
    upper = low_back(jnp.dot(normed_two, wu, precision=high))
    hidden = low(jax.nn.silu(gate) * upper)
    return middle + jnp.dot(hidden, wd, precision=high)

def reference(tokens, cotangent, gain_attn, gain_mlp, w_query, w_key, w_value, w_out, w_gate, w_up, w_down):
    params = tuple((w.astype(jnp.float32) for w in (gain_attn, gain_mlp, w_query, w_key, w_value, w_out, w_gate, w_up, w_down)))

    def per_sequence(total, pair):
        sequence, backward = pair
        result, pull = jax.vjp(layer, sequence.astype(jnp.float32), *params)
        grads = pull(backward.astype(jnp.float32))
        total = tuple((acc + new for acc, new in zip(total, grads[1:])))
        return (total, (result.astype(jnp.bfloat16), grads[0]))
    zeros = tuple((jnp.zeros(w.shape, jnp.float32) for w in params))
    total, (outputs, grad_in) = lax.scan(per_sequence, zeros, (tokens, cotangent))
    return (outputs, grad_in, total[0], total[1], total[2], total[3], total[4], total[5], total[6], total[7], total[8])
```

```python
import functools

import jax
import jax.numpy as jnp
import numpy as np
from jax import lax
from jax.experimental import pallas as pl
from jax.experimental.pallas import tpu as pltpu
from jax.sharding import PartitionSpec as P

D = 576
HEADS = 9
KV_HEADS = 3
HEAD = 64
GROUP = HEADS // KV_HEADS
FF = 1536
KV = KV_HEADS * HEAD
MESH = pl.DeviceIdType.MESH
BF = jnp.bfloat16
F32 = jnp.float32

EARLY = 48
LATE = 192
EARLY_STREAMS = ((0, 16, (0, 1, 2)), (16, 32, (1, 2, 0)), (32, 48, (2, 0, 1)))
LATE_GATHER = ((0, 80, (2, 1, 0)), (80, 160, (2, 0, 1)), (160, 192, (0, 1, 2)))
LATE_REDUCE = ((0, 80, (0, 1, 2)), (80, 160, (1, 0, 2)), (160, 192, (2, 0, 1)))
UP_AT, DOWN_AT, TAIL_AT, OUT_AT = 54, 112, 160, 168
VMEM_LIMIT = 60 * 1024 * 1024


class Place:
    def __init__(self, sides):
        self.sides = sides
        nx, ny, nz = sides
        self.low = nz // 2
        dp = lax.axis_index("dp")
        ctx = lax.axis_index("ctx")
        x = dp // (self.low * ny)
        y = dp % ny
        z = (ctx // 2) * self.low + (dp // ny) % self.low
        self.at = (x, y, z)
        self.core = ctx % 2

    def device(self, at, core):
        x, y, z = at
        dp = (x * self.low + z % self.low) * self.sides[1] + y
        return (dp, (z // self.low) * 2 + core)

    def shifted(self, axis, step):
        at = list(self.at)
        n = self.sides[axis]
        at[axis] = lax.rem(at[axis] + (step + n), n)
        return tuple(at)

    def peer(self, axis, step):
        return self.device(self.shifted(axis, step), self.core)

    def sibling(self):
        return self.device(self.at, 1 - self.core)


def greet(place):
    barrier = pltpu.get_barrier_semaphore()
    friends = [place.sibling()]
    for axis in range(3):
        for step in range(1, place.sides[axis]):
            friends.append(place.peer(axis, step))
    for friend in friends:
        pl.semaphore_signal(barrier, inc=1, device_id=friend, device_id_type=MESH)
    pl.semaphore_wait(barrier, len(friends))


def remote(src, dst, send_sem, recv_sem, device):
    return pltpu.make_async_remote_copy(
        src_ref=src,
        dst_ref=dst,
        send_sem=send_sem,
        recv_sem=recv_sem,
        device_id=device,
        device_id_type=MESH,
    )


class Gather:
    def __init__(self, place, streams, slot_ref, out_ref, sems):
        self.place, self.streams = place, streams
        self.slot_ref, self.out_ref = slot_ref, out_ref
        self.local_sem, self.send_sem, self.recv_sem, self.pair_send, self.pair_recv = sems
        self.sends = [[] for _ in streams]
        self.pairs = []

    def region(self, free, at, lo, hi):
        index = tuple(slice(None) if axis in free else at[axis] for axis in range(3))
        return self.out_ref.at[(self.place.core,) + index + (pl.ds(lo, hi - lo),)]

    def exchange(self, number, phase, src, free, axis, lo, hi):
        for step in range(1, self.place.sides[axis]):
            copy = remote(
                src,
                self.region(free, self.place.at, lo, hi),
                self.send_sem.at[number, phase, step - 1],
                self.recv_sem.at[number, phase, step - 1],
                self.place.peer(axis, step),
            )
            copy.start()
            self.sends[number].append(copy)

    def start(self):
        for number, (lo, hi, order) in enumerate(self.streams):
            src = self.slot_ref.at[pl.ds(lo, hi - lo)]
            self.exchange(number, 0, src, (), order[0], lo, hi)
        own = self.out_ref.at[(self.place.core,) + self.place.at]
        self.local = pltpu.make_async_copy(self.slot_ref, own, self.local_sem)
        self.local.start()

    def relay(self, number, step, at, lo, hi, order):
        plane = self.region(order[:2], at, lo, hi)
        copy = remote(
            plane,
            plane,
            self.pair_send.at[number, step],
            self.pair_recv.at[number, step],
            self.place.sibling(),
        )
        copy.start()
        self.pairs.append(copy)

    def phase(self, phase):
        if phase == 1:
            self.local.wait()
        for number, (lo, hi, order) in enumerate(self.streams):
            for copy in self.sends[number][-(self.place.sides[order[phase - 1]] - 1) :]:
                copy.wait_recv()
            free = order[:phase]
            src = self.region(free, self.place.at, lo, hi)
            self.exchange(number, phase, src, free, order[phase], lo, hi)
        if phase == 2:
            for number, (lo, hi, order) in enumerate(self.streams):
                self.relay(number, 0, self.place.at, lo, hi, order)

    def arrive(self, step):
        for number, (lo, hi, order) in enumerate(self.streams):
            axis = order[2]
            if step < self.place.sides[axis]:
                self.sends[number][step - self.place.sides[axis]].wait_recv()
                self.relay(number, step, self.place.shifted(axis, -step), lo, hi, order)

    def finish(self):
        for group in self.sends:
            for copy in group:
                copy.wait_send()
        for copy in self.pairs:
            copy.wait()


def gather_sems(sides, streams):
    n, side = len(streams), max(sides)
    return [
        pltpu.SemaphoreType.DMA,
        pltpu.SemaphoreType.DMA((n, 3, side - 1)),
        pltpu.SemaphoreType.DMA((n, 3, side - 1)),
        pltpu.SemaphoreType.DMA((n, side)),
        pltpu.SemaphoreType.DMA((n, side)),
    ]


class Reduce:
    def __init__(self, place, streams, grads_ref, out_ref, scratch):
        self.place, self.streams = place, streams
        self.grads_ref, self.out_ref = grads_ref, out_ref
        self.pair, self.first, self.second, self.third = scratch[:4]
        self.pair_send, self.pair_recv, self.send_sem, self.recv_sem = scratch[4:]
        self.side = place.sides[0]
        self.sends = [[] for _ in streams]

    def start(self):
        self.swaps = []
        core = self.place.core
        for number, (lo, hi, order) in enumerate(self.streams):
            rows = pl.ds(lo, hi - lo)
            copy = remote(
                self.grads_ref.at[1 - core, :, :, :, rows],
                self.pair.at[:, :, :, rows],
                self.pair_send.at[number],
                self.pair_recv.at[number],
                self.place.sibling(),
            )
            copy.start()
            self.swaps.append(copy)

    def place_of(self, order, coords):
        index = [None, None, None]
        for axis, coord in zip(order, coords):
            index[axis] = coord
        return tuple(index)

    def exchange(self, number, phase, buffers, order, lo, hi):
        rows = pl.ds(lo, hi - lo)
        place, axis = self.place, order[phase]
        for step in range(1, self.side):
            fixed = [place.at[order[i]] for i in range(phase)]
            coords = fixed + [place.shifted(axis, step)[axis]] + [slice(None)] * (2 - phase)
            copy = remote(
                self.grads_ref.at[(place.core,) + self.place_of(order, coords) + (rows,)],
                buffers.at[(step - 1,) + (slice(None),) * (2 - phase) + (rows,)],
                self.send_sem.at[number, phase, step - 1],
                self.recv_sem.at[number, phase, step - 1],
                place.peer(axis, step),
            )
            copy.start()
            self.sends[number].append(copy)

    def arrived(self, number, phase):
        for copy in self.sends[number][phase * (self.side - 1) : (phase + 1) * (self.side - 1)]:
            copy.wait_recv()

    def phase_pair(self):
        held, pair, side, core = self.grads_ref, self.pair, self.side, self.place.core
        for number, (lo, hi, order) in enumerate(self.streams):
            rows = pl.ds(lo, hi - lo)
            self.swaps[number].wait_recv()

            def add(i, carry, rows=rows):
                a, b = i // side, i % side
                for c in range(side):
                    at = (core, a, b, c, rows)
                    held[at] = (held[at].astype(F32) + pair[at[1:]].astype(F32)).astype(BF)
                return carry

            lax.fori_loop(0, side * side, add, 0)
            self.exchange(number, 0, self.first, order, lo, hi)

    def phase_first(self):
        held, first, side, place = self.grads_ref, self.first, self.side, self.place
        for number, (lo, hi, order) in enumerate(self.streams):
            rows = pl.ds(lo, hi - lo)
            self.arrived(number, 0)

            def add(i, carry, rows=rows, order=order):
                b, c = i // side, i % side
                axes = (order[0],) + tuple(sorted(order[1:]))
                at = self.place_of(axes, (place.at[order[0]], b, c)) + (rows,)
                at = (place.core,) + at
                total = held[at].astype(F32)
                for step in range(side - 1):
                    total += first[step, b, c, rows].astype(F32)
                held[at] = total.astype(BF)
                return carry

            lax.fori_loop(0, side * side, add, 0)
            self.exchange(number, 1, self.second, order, lo, hi)

    def phase_second(self):
        held, second, side, place = self.grads_ref, self.second, self.side, self.place
        for number, (lo, hi, order) in enumerate(self.streams):
            rows = pl.ds(lo, hi - lo)
            self.arrived(number, 1)

            def add(c, carry, rows=rows, order=order):
                at = self.place_of(order, (place.at[order[0]], place.at[order[1]], c)) + (rows,)
                at = (place.core,) + at
                total = held[at].astype(F32)
                for step in range(side - 1):
                    total += second[step, c, rows].astype(F32)
                held[at] = total.astype(BF)
                return carry

            lax.fori_loop(0, side, add, 0)
            self.exchange(number, 2, self.third, order, lo, hi)

    def finish(self):
        for number, (lo, hi, order) in enumerate(self.streams):
            rows = pl.ds(lo, hi - lo)
            self.arrived(number, 2)
            total = self.grads_ref[(self.place.core,) + self.place.at + (rows,)].astype(F32)
            for step in range(self.side - 1):
                total += self.third[step, rows].astype(F32)
            self.out_ref[rows] = total
        for copy in self.swaps:
            copy.wait_send()
        for group in self.sends:
            for copy in group:
                copy.wait_send()


def reduce_scratch(sides, rows, streams):
    n, side = len(streams), sides[0]
    return [
        pltpu.VMEM(sides + (rows, 128), BF),
        pltpu.VMEM((side - 1, side, side, rows, 128), BF),
        pltpu.VMEM((side - 1, side, rows, 128), BF),
        pltpu.VMEM((side - 1, rows, 128), BF),
        pltpu.SemaphoreType.DMA((n,)),
        pltpu.SemaphoreType.DMA((n,)),
        pltpu.SemaphoreType.DMA((n, 3, side - 1)),
        pltpu.SemaphoreType.DMA((n, 3, side - 1)),
    ]


def pack_rows(pieces, rows):
    have = sum(piece.shape[0] for piece in pieces)
    if have < rows:
        pieces = pieces + [jnp.zeros((rows - have, 128), pieces[0].dtype)]
    return jnp.concatenate(pieces, 0)


def thin(block, count):
    return [block[:, 128 * t : 128 * t + 128] for t in range(count)]


def down_tail(tail):
    pieces = [tail[8 * b : 8 * b + 8] for b in range(6)]
    return jnp.concatenate(pieces + [jnp.zeros((8, 32), tail.dtype)], 1)


def open_tail(part):
    return jnp.concatenate([part[:, 16 * b : 16 * b + 16] for b in range(6)], 0)


def pack_weights(wq, wk, wv, wo, wg, wu, wd, gains, early_ref, late_ref):
    f = lambda ref: ref[...].astype(F32)
    out = f(wo)
    small = jnp.concatenate([f(wq), f(wk), f(wv), out[:, 128:]], 1)
    gain = jnp.concatenate([f(ref) for ref in gains], 0)
    gain = jnp.concatenate([gain, jnp.zeros((2, 128 - gain.shape[1]), F32)], 1)
    early_ref[...] = pack_rows(thin(small, 2) + [gain], EARLY).astype(BF)
    down = f(wd)
    late_ref[0:DOWN_AT] = pack_rows(thin(f(wg), 3) + thin(f(wu), 3), DOWN_AT).astype(BF)
    late_ref[DOWN_AT:TAIL_AT] = down[:, :128].astype(BF)
    tail = pack_rows([down_tail(down[:, 128:]), out[:, :128]], LATE - TAIL_AT)
    late_ref[TAIL_AT:LATE] = tail.astype(BF)


def unpack_early(slots, wqkv, tails):
    def block(x, carry):
        smalls = []
        for ctx in range(4):
            zh, core = ctx // 2, ctx % 2
            small = []
            for i in range(8):
                small.append(slots[core, x, i % 4, zh * 2 + i // 4].astype(F32))
            stack = lambda t: jnp.concatenate([b[18 * t : 18 * t + 18] for b in small], 0)
            smalls.append(jnp.concatenate([stack(t) for t in range(2)], 1))
        cut = lambda lo, hi: [part[:, lo:hi] for part in smalls]
        rows = pl.ds(pl.multiple_of(144 * x, 16), 144)
        whole = jnp.concatenate(cut(0, 144) + cut(144, 192) + cut(192, 240), 1)
        wqkv[rows, :] = whole.astype(BF)
        tails[rows, :] = jnp.concatenate(cut(240, 256), 1)
        return carry

    lax.fori_loop(0, 4, block, 0)


def unpack_gains(slots):
    pieces = []
    for x in range(4):
        for i in range(8):
            tile = slots[0, x, i % 4, i // 4, 32:48, :].astype(F32)
            pieces.append(tile[4:6, :18])
    return jnp.concatenate(pieces, 1)


def unpack_late(slots, tails, wo, wg, wu, wd):
    def block(x, carry):
        downs, outs = [[] for _ in range(8)], []
        rows = pl.ds(pl.multiple_of(144 * x, 16), 144)
        for ctx in range(4):
            zh, core = ctx // 2, ctx % 2
            gate, up, out = [], [], []
            for i in range(8):
                at = (core, x, i % 4, zh * 2 + i // 4)
                slot = slots[at].astype(F32)
                gate.append(slot[:UP_AT])
                up.append(slot[UP_AT : 2 * UP_AT])
                out.append(slot[OUT_AT : OUT_AT + 18])
                downs[i] += [slot[DOWN_AT:TAIL_AT], open_tail(slot[TAIL_AT:OUT_AT])]
            for t in range(3):
                lanes = slice(ctx * 384 + 128 * t, ctx * 384 + 128 * t + 128)
                stack = lambda blocks: jnp.concatenate(
                    [b[18 * t : 18 * t + 18] for b in blocks], 0
                )
                wg[rows, lanes] = stack(gate).astype(BF)
                wu[rows, lanes] = stack(up).astype(BF)
            outs += [jnp.concatenate(out, 0), tails[rows, 16 * ctx : 16 * ctx + 16]]
        wo[rows, :] = jnp.concatenate(outs, 1).astype(BF)
        for i in range(8):
            at = pl.ds(pl.multiple_of(384 * x + 48 * i, 16), 48)
            wd[at, :] = jnp.concatenate(downs[i], 1).astype(BF)
        return carry

    lax.fori_loop(0, 4, block, 0)


def pack_wide(gg, gu, chunk, slots):
    zh, core = chunk // 2, chunk % 2

    def block(x, carry):
        rows = pl.ds(pl.multiple_of(144 * x, 16), 144)
        gate, up = gg[rows, :], gu[rows, :]
        for i in range(8):
            at = slice(18 * i, 18 * i + 18)
            slot = pack_rows(thin(gate[at], 3) + thin(up[at], 3), DOWN_AT).astype(BF)
            slots[core, x, i % 4, zh * 2 + i // 4, 0:DOWN_AT] = slot
        return carry

    lax.fori_loop(0, 4, block, 0)


def pack_down(gd, x, slots, tails):
    for ctx in range(4):
        zh, core = ctx // 2, ctx % 2
        for i in range(8):
            part = gd[48 * i : 48 * i + 48, 144 * ctx : 144 * ctx + 144]
            slots[core, x, i % 4, zh * 2 + i // 4, DOWN_AT:TAIL_AT] = part[:, :128].astype(BF)
            tails[x, i, ctx] = down_tail(part[:, 128:])


def pack_out(go, tails, slots):
    def block(x, carry):
        out = go[pl.ds(pl.multiple_of(144 * x, 16), 144), :]
        for ctx in range(4):
            zh, core = ctx // 2, ctx % 2
            main = out[:, 144 * ctx : 144 * ctx + 128]
            for i in range(8):
                pieces = [tails[x, i, ctx], main[18 * i : 18 * i + 18]]
                slot = pack_rows(pieces, LATE - TAIL_AT).astype(BF)
                slots[core, x, i % 4, zh * 2 + i // 4, TAIL_AT:LATE] = slot
        return carry

    lax.fori_loop(0, 4, block, 0)


def pack_early(gqkv, go, gains, out_ref):
    def block(x, carry):
        rows = pl.ds(pl.multiple_of(144 * x, 16), 144)
        whole = gqkv[rows, :]
        out = go[rows, :]
        for ctx in range(4):
            zh, core = ctx // 2, ctx % 2
            small = jnp.concatenate(
                [
                    whole[:, 144 * ctx : 144 * ctx + 144],
                    whole[:, D + 48 * ctx : D + 48 * ctx + 48],
                    whole[:, D + KV + 48 * ctx : D + KV + 48 * ctx + 48],
                    out[:, 144 * ctx + 128 : 144 * ctx + 144],
                ],
                1,
            )
            for i in range(8):
                pieces = thin(small[18 * i : 18 * i + 18], 2) + [gains[x, i]]
                slot = pack_rows(pieces, EARLY).astype(BF)
                out_ref[core, x, i % 4, zh * 2 + i // 4] = slot
        return carry

    lax.fori_loop(0, 4, block, 0)


def finish_kernel(early, late, out, dx, out_to, dx_to, ga, gm, gq, gk, gv, go, gg, gu, gd):
    def wide(slot, base, count):
        return jnp.concatenate(
            [slot[base + 18 * t : base + 18 * t + 18] for t in range(count)], 1
        )

    gg[...] = wide(late, 0, 3)
    gu[...] = wide(late, UP_AT, 3)
    gd[...] = jnp.concatenate([late[DOWN_AT:TAIL_AT], open_tail(late[TAIL_AT:OUT_AT])], 1)
    small = wide(early, 0, 2)
    gq[...] = small[:, :144]
    gk[...] = small[:, 144:192]
    gv[...] = small[:, 192:240]
    go[...] = jnp.concatenate([late[OUT_AT : OUT_AT + 18], small[:, 240:256]], 1)
    ga[...] = early[36:37, :18]
    gm[...] = early[37:38, :18]
    out_to[...] = out[...]
    dx_to[...] = dx[...]


def three_heads(ref, g, half, size):
    lanes = slice(half * size, half * size + size)
    base = g * GROUP * HEAD
    heads = [ref[base + HEAD * j : base + HEAD * j + HEAD, lanes] for j in range(GROUP)]
    return jnp.concatenate(heads, 1)


def turn(vectors, cosine, sine):
    first, second = vectors[: HEAD // 2], vectors[HEAD // 2 :]
    return jnp.concatenate([first * cosine - second * sine, second * cosine + first * sine], 0)


def columns_of(rows):
    full = jnp.concatenate([rows, jnp.zeros((2, 64), F32)], 1)
    turned = jnp.concatenate([full, jnp.zeros((126, 640), F32)], 0).T
    return turned[:D, 0:1], turned[:D, 1:2]


def rows_of(first, second):
    lane = lax.broadcasted_iota(jnp.int32, (D, 128), 1)
    full = jnp.where(lane == 0, first, jnp.where(lane == 1, second, 0.0))
    full = jnp.concatenate([full, jnp.zeros((64, 128), F32)], 0)
    return full.T[0:2, :D]


def causal(size):
    key = lax.broadcasted_iota(jnp.int32, (size, GROUP * size), 0)
    query = lax.broadcasted_iota(jnp.int32, (size, GROUP * size), 1) % size
    return key <= query


def mul(a, b, ca, cb):
    return lax.dot_general(a, b, (((ca,), (cb,)), ((), ())), preferred_element_type=F32)


class Context:
    def __init__(self, place, size):
        ctx = lax.axis_index("ctx")
        half, core = ctx // 2, ctx % 2
        self.size = size
        self.me = ctx
        self.sibling = half * 2 + 1 - core
        self.partner = (1 - half) * 2 + core
        self.corner = (1 - half) * 2 + 1 - core
        self.sibling_device = place.sibling()
        self.partner_device = place.peer(2, place.sides[2] // 2)

    def pairs(self, owner):
        late = jnp.where(owner > self.me, 1, 0)
        first, second = 1, late
        return (first, pl.ds(0, self.size)), (
            second,
            pl.ds(pl.multiple_of(late * self.size, self.size), self.size),
        )


def layer_kernel(sides, early_streams, late_gather, late_reduce, *refs):
    x_ref, dy_ref, wq, wk, wv, wo_ref, wg_ref, wu_ref, wd_ref = refs[:9]
    gain_a, gain_b, cos_ref, sin_ref = refs[9:13]
    out_ref, dx_ref, early_ref, total_ref = refs[13:17]
    scratch = refs[17:]
    early_slot, late_slot, early_slots, late_slots, kv_ref, kv_all = scratch[:6]
    queries, tops, totals, mixes, grads, lses, deltas, dqs = scratch[6:14]
    mixed_ref, normed_ref, wqkv, wo, wg, wu, wd, tails = scratch[14:22]
    middle, dmiddle, high, rising, falling, gate_grad, up_grad = scratch[22:29]
    out_grad, down_tails, acc, sent, passed, got, dqkv, gqkv, gain_rows = scratch[29:38]
    dy_rows = scratch[69]
    kv_sem, kv_send, kv_recv, back_send, back_recv = scratch[38:43]
    early_sems, late_sems = scratch[43:48], scratch[48:53]
    late_scratch, early_scratch = scratch[53:61], scratch[61:69]
    size = x_ref.shape[1] // 2
    place = Place(sides)
    ctx = Context(place, size)
    pack_weights(
        wq, wk, wv, wo_ref, wg_ref, wu_ref, wd_ref, (gain_a, gain_b), early_slot, late_slot
    )
    greet(place)
    early = Gather(place, early_streams, early_slot, early_slots, early_sems)
    gather = Gather(place, late_gather, late_slot, late_slots, late_sems)
    early.start()
    gather.start()

    def scale_of(values):
        return lax.rsqrt(jnp.mean(values * values, 0, keepdims=True) + 1e-05)

    inputs = x_ref[...].astype(F32)
    scale_one = scale_of(inputs)
    middle[...] = inputs * scale_one
    early.phase(1)
    gather.phase(1)
    early.phase(2)
    dy_rows[...] = dy_ref[...].astype(F32).T.astype(BF)
    for step in range(1, max(sides)):
        early.arrive(step)
    gather.phase(2)
    early.finish()
    unpack_early(early_slots, wqkv, tails)
    gain_one, gain_two = columns_of(unpack_gains(early_slots))
    normed_ref[...] = (middle[...] * gain_one).astype(BF)
    tables = [(cos_ref[b], sin_ref[b]) for b in (ctx.me, 7 - ctx.me)]
    pre = mul(wqkv[:, D:], normed_ref[...], 0, 0)
    for g in range(KV_HEADS):
        for half in range(2):
            lanes = slice(half * size, half * size + size)
            key = turn(pre[HEAD * g : HEAD * g + HEAD, lanes], *tables[half])
            both = jnp.concatenate([key, pre[KV + HEAD * g : KV + HEAD * g + HEAD, lanes]], 0)
            kv_ref[g, lanes, :] = both.T.astype(BF)
    far, near, corner = [], [], []
    for g in range(KV_HEADS):
        mine = kv_all.at[ctx.me, g]
        copy = remote(kv_ref.at[g], mine, kv_send.at[0, g], kv_recv.at[0, g], ctx.partner_device)
        copy.start()
        far.append(copy)
    for g in range(KV_HEADS):
        mine = kv_all.at[ctx.me, g]
        copy = remote(kv_ref.at[g], mine, kv_send.at[1, g], kv_recv.at[1, g], ctx.sibling_device)
        copy.start()
        near.append(copy)
    own = pltpu.make_async_copy(kv_ref, kv_all.at[ctx.me], kv_sem)
    own.start()
    for g in range(KV_HEADS):
        columns = slice(g * GROUP * HEAD, (g + 1) * GROUP * HEAD)
        pre = mul(wqkv[:, columns], normed_ref[...], 0, 0)
        for j in range(GROUP):
            for half in range(2):
                lanes = slice(half * size, half * size + size)
                turned = turn(pre[HEAD * j : HEAD * j + HEAD, lanes], *tables[half])
                turned = (turned * HEAD**-0.5).astype(BF)
                queries[g, half, :, size * j : size * j + size] = turned

    mask = causal(size)

    def scores_of(part):
        g, half, kv, masked = part[:4]
        scores = mul(kv[:, :HEAD], queries[g, half], 1, 0)
        return jnp.where(mask, scores, -1e30) if masked else scores

    def attend(parts):
        ahead = scores_of(parts[0])
        for n, (g, half, kv, masked, fresh) in enumerate(parts):
            scores = ahead
            if n + 1 < len(parts):
                ahead = scores_of(parts[n + 1])
            top = jnp.max(scores, 0, keepdims=True)
            if not fresh:
                before = tops[g, half]
                top = jnp.maximum(before, top)
            probs = jnp.exp(scores - top)
            total = jnp.sum(probs, 0, keepdims=True)
            mixed = mul(kv[:, HEAD:], probs.astype(BF), 0, 0)
            if not fresh:
                fade = jnp.exp(before - top)
                total += totals[g, half] * fade
                mixed += mixes[g, half] * fade
            tops[g, half], totals[g, half], mixes[g, half] = top, total, mixed

    def other(owner):
        parts = []
        for g in range(KV_HEADS):
            for half, rows in ctx.pairs(owner):
                parts.append((g, half, kv_all[owner, g, rows, :], False, False))
        attend(parts)

    parts = []
    for g in range(KV_HEADS):
        first, second = kv_ref[g, :size, :], kv_ref[g, size:, :]
        parts.append((g, 0, first, True, True))
        parts.append((g, 1, first, False, True))
        parts.append((g, 1, second, True, False))
    attend(parts)
    for copy in near:
        copy.wait_recv()
    other(ctx.sibling)
    for g in range(KV_HEADS):
        far[g].wait_recv()
        block = kv_all.at[ctx.partner, g]
        copy = remote(block, block, kv_send.at[2, g], kv_recv.at[2, g], ctx.sibling_device)
        copy.start()
        corner.append(copy)
    gather.arrive(1)
    other(ctx.partner)
    gather.arrive(2)
    for copy in corner:
        copy.wait_recv()
    own.wait()
    gather.arrive(3)
    other(ctx.corner)
    for g in range(KV_HEADS):
        for half in range(2):
            total = totals[g, half]
            mixed = (mixes[g, half] / total).astype(BF)
            lses[g, half] = tops[g, half] + jnp.log(total)
            lanes = slice(half * size, half * size + size)
            for j in range(GROUP):
                at = HEAD * (GROUP * g + j)
                mixed_ref[at : at + HEAD, lanes] = mixed[:, size * j : size * j + size]
    gather.finish()
    for copy in far + near + corner:
        copy.wait_send()

    unpack_late(late_slots, tails, wo, wg, wu, wd)
    middle[...] = x_ref[...].astype(F32) + mul(wo[...], mixed_ref[...], 0, 0)
    scale_two = scale_of(middle[...])
    normed_two = middle[...] * scale_two * gain_two
    high[...] = normed_two.astype(BF)
    low = normed_two.T.astype(BF)
    dy = dy_rows[...]
    rising[...] = jnp.zeros_like(rising)
    falling[...] = jnp.zeros_like(falling)

    def chunk(c, carry):
        lanes = pl.ds(pl.multiple_of(384 * c, 128), 384)
        gate_w, up_w, down_w = wg[:, lanes], wu[:, lanes], wd[lanes, :]
        gate = mul(low, gate_w, 1, 0)
        upper = mul(low, up_w, 1, 0)
        dhid = mul(dy, down_w, 1, 1)
        sigma = jax.nn.sigmoid(gate)
        silu = gate * sigma
        hidden = (silu * upper).astype(BF)
        dgate = (dhid * upper * sigma * (1.0 + gate * (1.0 - sigma))).astype(BF)
        dup = (dhid * silu).astype(BF)
        rising[...] += mul(hidden, down_w, 1, 0)
        falling[...] += mul(dgate, gate_w, 1, 1) + mul(dup, up_w, 1, 1)
        gate_grad[...] = mul(high[...], dgate, 1, 0)
        up_grad[...] = mul(high[...], dup, 1, 0)
        pack_wide(gate_grad, up_grad, c, late_slots)
        pack_down(mul(hidden, dy, 0, 0), c, late_slots, down_tails)
        return carry

    lax.fori_loop(0, 4, chunk, 0)
    out_ref[...] = (middle[...] + rising[...].T).astype(BF)
    grad = falling[...].T
    gain_grad_two = jnp.sum(grad * middle[...] * scale_two, 1, keepdims=True)
    gained = grad * gain_two
    dmiddle[...] = (
        dy_ref[...].astype(F32)
        + scale_two * gained
        - middle[...] * scale_two**3 * jnp.mean(middle[...] * gained, 0, keepdims=True)
    )
    dattn = dmiddle[...].astype(BF)
    out_grad[...] = mul(mixed_ref[...], dattn, 1, 1)
    pack_out(out_grad, down_tails, late_slots)
    reduce = Reduce(place, late_reduce, late_slots, total_ref, late_scratch)
    late_early = Reduce(place, early_streams, early_slots, early_ref, early_scratch)
    reduce.start()
    dmixed = mul(wo[...], dattn, 1, 0).astype(BF)
    for g in range(KV_HEADS):
        for half in range(2):
            grad = three_heads(dmixed, g, half, size)
            grads[g, half] = grad
            mixed = three_heads(mixed_ref, g, half, size)
            deltas[g, half] = jnp.sum(grad.astype(F32) * mixed.astype(F32), 0, keepdims=True)
    dqs[...] = jnp.zeros_like(dqs)

    def lead(part):
        g, half, kv, masked = part[:4]
        return scores_of(part), mul(kv[:, HEAD:], grads[g, half], 1, 0)

    def retrace(parts, give):
        ahead = lead(parts[0])
        for n, part in enumerate(parts):
            g, half, kv, masked = part
            scores, dprobs = ahead
            if n + 1 < len(parts):
                ahead = lead(parts[n + 1])
            probs = jnp.exp(scores - lses[g, half])
            dscores = (probs * (dprobs - deltas[g, half])).astype(BF)
            dvalue = mul(probs.astype(BF), grads[g, half], 1, 1)
            dkey = mul(dscores, queries[g, half], 1, 1)
            dqs[g, half] += mul(kv[:, :HEAD], dscores, 0, 0)
            give(n, g, jnp.concatenate([dkey, dvalue], 1))

    def back(owner, store):
        parts = []
        for g in range(KV_HEADS):
            for half, rows in ctx.pairs(owner):
                parts.append((g, half, kv_all[owner, g, rows, :], False))
        late = jnp.full((size, 128), owner, jnp.int32) > ctx.me
        kept = []

        def give(n, g, dkv):
            kept.append(dkv)
            if n % 2 == 1:
                store(g, kept[-2] + jnp.where(late, 0.0, dkv), jnp.where(late, dkv, 0.0))

        retrace(parts, give)

    def to_sibling(slot):
        def store(g, first, second):
            sent[slot, g, :size] = first.astype(BF)
            sent[slot, g, size:] = second.astype(BF)

        return store

    def to_acc(g, first, second):
        acc[g, :size] = first
        acc[g, size:] = second

    def send(slot):
        copies = []
        for g in range(KV_HEADS):
            copy = remote(
                sent.at[slot, g],
                got.at[slot, g],
                back_send.at[slot, g],
                back_recv.at[slot, g],
                ctx.sibling_device,
            )
            copy.start()
            copies.append(copy)
        return copies

    back(ctx.corner, to_sibling(0))
    copies = send(0)
    back(ctx.partner, to_acc)
    for copy in copies:
        copy.wait_recv()
    far = []
    for g in range(KV_HEADS):
        passed[g] = (acc[g] + got[0, g].astype(F32)).astype(BF)
        copy = remote(
            passed.at[g], got.at[2, g], back_send.at[2, g], back_recv.at[2, g], ctx.partner_device
        )
        copy.start()
        far.append(copy)
    reduce.phase_pair()
    back(ctx.sibling, to_sibling(1))
    near = send(1)
    parts, kept = [], []
    for g in range(KV_HEADS):
        first, second = kv_all[ctx.me, g, :size, :], kv_all[ctx.me, g, size:, :]
        parts += [(g, 0, first, True), (g, 1, first, False), (g, 1, second, True)]

    def keep(n, g, dkv):
        kept.append(dkv)
        if n % 3 == 2:
            to_acc(g, kept[-3] + kept[-2], dkv)

    retrace(parts, keep)
    for g in range(KV_HEADS):
        for half in range(2):
            lanes = slice(half * size, half * size + size)
            cosine, sine = tables[half]
            for j in range(GROUP):
                dquery = dqs[g, half, :, size * j : size * j + size] * HEAD**-0.5
                at = HEAD * (GROUP * g + j)
                dqkv[at : at + HEAD, lanes] = turn(dquery, cosine, -sine).astype(BF)
    for g in range(KV_HEADS):
        near[g].wait_recv()
        far[g].wait_recv()
        whole = (acc[g] + got[1, g].astype(F32) + got[2, g].astype(F32)).T
        at = D + HEAD * g
        for half in range(2):
            lanes = slice(half * size, half * size + size)
            cosine, sine = tables[half]
            dqkv[at : at + HEAD, lanes] = turn(whole[:HEAD, lanes], cosine, -sine).astype(BF)
        dqkv[at + KV : at + KV + HEAD, :] = whole[HEAD:].astype(BF)
    gqkv[...] = mul(normed_ref[...], dqkv[...], 1, 1)
    grad = mul(wqkv[...], dqkv[...], 1, 0)
    inputs = x_ref[...].astype(F32)
    scale_one = scale_of(inputs)
    gain_grad_one = jnp.sum(grad * inputs * scale_one, 1, keepdims=True)
    gain_grads = rows_of(gain_grad_one, gain_grad_two)
    for x in range(4):
        for i in range(8):
            at = 18 * (8 * x + i)
            gain_rows[x, i, :, 0:18] = gain_grads[:, at : at + 18]
    pack_early(gqkv, out_grad, gain_rows, early_slots)
    late_early.start()
    gained = grad * gain_one
    dx_ref[...] = (
        dmiddle[...]
        + scale_one * gained
        - inputs * scale_one**3 * jnp.mean(inputs * gained, 0, keepdims=True)
    )
    reduce.phase_first()
    late_early.phase_pair()
    reduce.phase_second()
    late_early.phase_first()
    late_early.phase_second()
    reduce.finish()
    late_early.finish()
    for copy in copies + far + near:
        copy.wait_send()


def layer(tokens, cotangent, weights, gains, sides):
    rows = tokens.shape[1]
    size = rows // 2
    vmem = pl.BlockSpec(memory_space=pltpu.VMEM)
    wide = GROUP * size
    kv = (KV_HEADS, rows, 2 * HEAD)
    heads = lambda height, kind: pltpu.VMEM((KV_HEADS, 2, height, wide), kind)
    dma = pltpu.SemaphoreType.DMA
    return pl.pallas_call(
        functools.partial(layer_kernel, sides, EARLY_STREAMS, LATE_GATHER, LATE_REDUCE),
        out_shape=[
            jax.ShapeDtypeStruct((D, rows), BF),
            jax.ShapeDtypeStruct((D, rows), F32),
            jax.ShapeDtypeStruct((EARLY, 128), F32),
            jax.ShapeDtypeStruct((LATE, 128), F32),
        ],
        in_specs=[vmem] * 13,
        out_specs=[vmem] * 4,
        scratch_shapes=[
            pltpu.VMEM((EARLY, 128), BF),
            pltpu.VMEM((LATE, 128), BF),
            pltpu.VMEM((2,) + sides + (EARLY, 128), BF),
            pltpu.VMEM((2,) + sides + (LATE, 128), BF),
            pltpu.VMEM(kv, BF),
            pltpu.VMEM((4,) + kv, BF),
            heads(HEAD, BF),
            heads(1, F32),
            heads(1, F32),
            heads(HEAD, F32),
            heads(HEAD, BF),
            heads(1, F32),
            heads(1, F32),
            heads(HEAD, F32),
            pltpu.VMEM((D, rows), BF),
            pltpu.VMEM((D, rows), BF),
            pltpu.VMEM((D, D + 2 * KV), BF),
            pltpu.VMEM((D, D), BF),
            pltpu.VMEM((D, FF), BF),
            pltpu.VMEM((D, FF), BF),
            pltpu.VMEM((FF, D), BF),
            pltpu.VMEM((D, 64), F32),
            pltpu.VMEM((D, rows), F32),
            pltpu.VMEM((D, rows), F32),
            pltpu.VMEM((D, rows), BF),
            pltpu.VMEM((rows, D), F32),
            pltpu.VMEM((rows, D), F32),
            pltpu.VMEM((D, FF // 4), F32),
            pltpu.VMEM((D, FF // 4), F32),
            pltpu.VMEM((D, D), F32),
            pltpu.VMEM((4, 8, 4, 8, 128), F32),
            pltpu.VMEM(kv, F32),
            pltpu.VMEM((2,) + kv, BF),
            pltpu.VMEM(kv, BF),
            pltpu.VMEM((3,) + kv, BF),
            pltpu.VMEM((D + 2 * KV, rows), BF),
            pltpu.VMEM((D, D + 2 * KV), F32),
            pltpu.VMEM((4, 8, 2, 128), F32),
            dma,
            dma((3, KV_HEADS)),
            dma((3, KV_HEADS)),
            dma((3, KV_HEADS)),
            dma((3, KV_HEADS)),
        ]
        + gather_sems(sides, EARLY_STREAMS)
        + gather_sems(sides, LATE_GATHER)
        + reduce_scratch(sides, LATE, LATE_REDUCE)
        + reduce_scratch(sides, EARLY, EARLY_STREAMS)
        + [pltpu.VMEM((rows, D), BF)],
        compiler_params=pltpu.CompilerParams(
            collective_id=0, has_side_effects=True, vmem_limit_bytes=VMEM_LIMIT
        ),
        name="decoder_layer",
    )(tokens, cotangent, *weights, *gains, *angles(size))


def angles(size):
    freq = 100000.0 ** (-np.arange(HEAD // 2) * 2.0 / HEAD)
    pos = np.arange(8 * size).reshape(8, 1, size)
    angle = pos * freq[None, :, None]
    return jnp.asarray(np.cos(angle), F32), jnp.asarray(np.sin(angle), F32)


def shards(
    tokens, cotangent, gain_attn, gain_mlp, w_query, w_key, w_value, w_out, w_gate, w_up, w_down
):
    sides = (4, 4, 4)
    result, grad_inputs, early_total, late_total = layer(
        tokens[0].T,
        cotangent[0].T,
        (w_query, w_key, w_value, w_out, w_gate, w_up, w_down),
        (gain_attn[None], gain_mlp[None]),
        sides,
    )
    shapes = [(1, 18), (1, 18), (18, 144), (18, 48), (18, 48), (18, 144), (18, 384), (18, 384)]
    out, dx, ga, gm, *grads = pl.pallas_call(
        finish_kernel,
        out_shape=[
            jax.ShapeDtypeStruct(result.shape, BF),
            jax.ShapeDtypeStruct(grad_inputs.shape, F32),
        ]
        + [jax.ShapeDtypeStruct(shape, F32) for shape in shapes + [(48, 144)]],
        name="finish",
    )(early_total, late_total, result, grad_inputs)
    return (out.T[None], dx.T[None], ga[0], gm[0], *grads)


def solution(mesh):
    both = P("dp", "ctx")
    block = P("dp", "ctx", None)
    return jax.shard_map(
        shards,
        mesh=mesh,
        in_specs=(block, block, P("dp"), P("dp")) + (both,) * 7,
        out_specs=(block, block, P("dp"), P("dp")) + (both,) * 7,
        check_vma=False,
    )
```

```python
import functools

import jax
import jax.numpy as jnp
import numpy as np
from jax import lax
from jax.experimental import pallas as pl
from jax.experimental.pallas import tpu as pltpu
from jax.sharding import PartitionSpec as P

D = 576
HEADS = 9
KV_HEADS = 3
HEAD = 64
GROUP = HEADS // KV_HEADS
FF = 1536
KV = KV_HEADS * HEAD
MESH = pl.DeviceIdType.MESH
BF = jnp.bfloat16
F32 = jnp.float32

EARLY = 48
LATE = 192
EARLY_STREAMS = ((0, 16, (0, 1, 2)), (16, 32, (1, 2, 0)), (32, 48, (2, 0, 1)))
LATE_GATHER = ((0, 80, (2, 1, 0)), (80, 160, (2, 0, 1)), (160, 192, (0, 1, 2)))
LATE_REDUCE = ((0, 80, (0, 1, 2)), (80, 160, (1, 0, 2)), (160, 192, (2, 0, 1)))
UP_AT, DOWN_AT, TAIL_AT, OUT_AT = 54, 112, 160, 168
VMEM_LIMIT = 60 * 1024 * 1024


class Place:
    def __init__(self, sides):
        self.sides = sides
        nx, ny, nz = sides
        self.low = nz // 2
        dp = lax.axis_index("dp")
        ctx = lax.axis_index("ctx")
        x = dp // (self.low * ny)
        y = dp % ny
        z = (ctx // 2) * self.low + (dp // ny) % self.low
        self.at = (x, y, z)
        self.core = ctx % 2

    def device(self, at, core):
        x, y, z = at
        dp = (x * self.low + z % self.low) * self.sides[1] + y
        return (dp, (z // self.low) * 2 + core)

    def shifted(self, axis, step):
        at = list(self.at)
        n = self.sides[axis]
        at[axis] = lax.rem(at[axis] + (step + n), n)
        return tuple(at)

    def peer(self, axis, step):
        return self.device(self.shifted(axis, step), self.core)

    def sibling(self):
        return self.device(self.at, 1 - self.core)


def greet(place):
    barrier = pltpu.get_barrier_semaphore()
    friends = [place.sibling()]
    for axis in range(3):
        for step in range(1, place.sides[axis]):
            friends.append(place.peer(axis, step))
    for friend in friends:
        pl.semaphore_signal(barrier, inc=1, device_id=friend, device_id_type=MESH)
    pl.semaphore_wait(barrier, len(friends))


def remote(src, dst, send_sem, recv_sem, device):
    return pltpu.make_async_remote_copy(
        src_ref=src,
        dst_ref=dst,
        send_sem=send_sem,
        recv_sem=recv_sem,
        device_id=device,
        device_id_type=MESH,
    )


class Gather:
    def __init__(self, place, streams, slot_ref, out_ref, sems):
        self.place, self.streams = place, streams
        self.slot_ref, self.out_ref = slot_ref, out_ref
        self.local_sem, self.send_sem, self.recv_sem, self.pair_send, self.pair_recv = sems
        self.sends = [[] for _ in streams]
        self.pairs = []

    def region(self, free, at, lo, hi):
        index = tuple(slice(None) if axis in free else at[axis] for axis in range(3))
        return self.out_ref.at[(self.place.core,) + index + (pl.ds(lo, hi - lo),)]

    def exchange(self, number, phase, src, free, axis, lo, hi):
        for step in range(1, self.place.sides[axis]):
            copy = remote(
                src,
                self.region(free, self.place.at, lo, hi),
                self.send_sem.at[number, phase, step - 1],
                self.recv_sem.at[number, phase, step - 1],
                self.place.peer(axis, step),
            )
            copy.start()
            self.sends[number].append(copy)

    def start(self):
        for number, (lo, hi, order) in enumerate(self.streams):
            src = self.slot_ref.at[pl.ds(lo, hi - lo)]
            self.exchange(number, 0, src, (), order[0], lo, hi)
        own = self.out_ref.at[(self.place.core,) + self.place.at]
        self.local = pltpu.make_async_copy(self.slot_ref, own, self.local_sem)
        self.local.start()

    def relay(self, number, step, at, lo, hi, order):
        plane = self.region(order[:2], at, lo, hi)
        copy = remote(
            plane,
            plane,
            self.pair_send.at[number, step],
            self.pair_recv.at[number, step],
            self.place.sibling(),
        )
        copy.start()
        self.pairs.append(copy)

    def phase(self, phase):
        if phase == 1:
            self.local.wait()
        for number, (lo, hi, order) in enumerate(self.streams):
            for copy in self.sends[number][-(self.place.sides[order[phase - 1]] - 1) :]:
                copy.wait_recv()
            free = order[:phase]
            src = self.region(free, self.place.at, lo, hi)
            self.exchange(number, phase, src, free, order[phase], lo, hi)
        if phase == 2:
            for number, (lo, hi, order) in enumerate(self.streams):
                self.relay(number, 0, self.place.at, lo, hi, order)

    def arrive(self, step):
        for number, (lo, hi, order) in enumerate(self.streams):
            axis = order[2]
            if step < self.place.sides[axis]:
                self.sends[number][step - self.place.sides[axis]].wait_recv()
                self.relay(number, step, self.place.shifted(axis, -step), lo, hi, order)

    def finish(self):
        for group in self.sends:
            for copy in group:
                copy.wait_send()
        for copy in self.pairs:
            copy.wait()


def gather_sems(sides, streams):
    n, side = len(streams), max(sides)
    return [
        pltpu.SemaphoreType.DMA,
        pltpu.SemaphoreType.DMA((n, 3, side - 1)),
        pltpu.SemaphoreType.DMA((n, 3, side - 1)),
        pltpu.SemaphoreType.DMA((n, side)),
        pltpu.SemaphoreType.DMA((n, side)),
    ]


class Reduce:
    def __init__(self, place, streams, grads_ref, out_ref, scratch):
        self.place, self.streams = place, streams
        self.grads_ref, self.out_ref = grads_ref, out_ref
        self.pair, self.first, self.second, self.third = scratch[:4]
        self.pair_send, self.pair_recv, self.send_sem, self.recv_sem = scratch[4:]
        self.side = place.sides[0]
        self.sends = [[] for _ in streams]

    def swap(self, index, at):
        return remote(
            self.grads_ref.at[(1 - self.place.core,) + at],
            self.pair.at[at],
            self.pair_send.at[index],
            self.pair_recv.at[index],
            self.place.sibling(),
        )

    def start(self):
        self.swaps = []
        for number, (lo, hi, order) in enumerate(self.streams):
            copy = self.swap(number, (slice(None),) * 3 + (pl.ds(lo, hi - lo),))
            copy.start()
            self.swaps.append([copy])

    def place_of(self, order, coords):
        index = [None, None, None]
        for axis, coord in zip(order, coords):
            index[axis] = coord
        return tuple(index)

    def exchange(self, number, phase, buffers, order, lo, hi):
        rows = pl.ds(lo, hi - lo)
        place, axis = self.place, order[phase]
        for step in range(1, self.side):
            fixed = [place.at[order[i]] for i in range(phase)]
            coords = fixed + [place.shifted(axis, step)[axis]] + [slice(None)] * (2 - phase)
            copy = remote(
                self.grads_ref.at[(place.core,) + self.place_of(order, coords) + (rows,)],
                buffers.at[(step - 1,) + (slice(None),) * (2 - phase) + (rows,)],
                self.send_sem.at[number, phase, step - 1],
                self.recv_sem.at[number, phase, step - 1],
                place.peer(axis, step),
            )
            copy.start()
            self.sends[number].append(copy)

    def arrived(self, number, phase):
        for copy in self.sends[number][phase * (self.side - 1) : (phase + 1) * (self.side - 1)]:
            copy.wait_recv()

    def phase_pair(self):
        held, pair, side, core = self.grads_ref, self.pair, self.side, self.place.core
        for number, (lo, hi, order) in enumerate(self.streams):
            rows = pl.ds(lo, hi - lo)
            for copy in self.swaps[number]:
                copy.wait_recv()

            def add(i, carry, rows=rows):
                a, b = i // side, i % side
                for c in range(side):
                    at = (core, a, b, c, rows)
                    held[at] = (held[at].astype(F32) + pair[at[1:]].astype(F32)).astype(BF)
                return carry

            lax.fori_loop(0, side * side, add, 0)
            self.exchange(number, 0, self.first, order, lo, hi)

    def phase_first(self):
        held, first, side, place = self.grads_ref, self.first, self.side, self.place
        for number, (lo, hi, order) in enumerate(self.streams):
            rows = pl.ds(lo, hi - lo)
            self.arrived(number, 0)

            def add(i, carry, rows=rows, order=order):
                b, c = i // side, i % side
                axes = (order[0],) + tuple(sorted(order[1:]))
                at = self.place_of(axes, (place.at[order[0]], b, c)) + (rows,)
                at = (place.core,) + at
                total = held[at].astype(F32)
                for step in range(side - 1):
                    total += first[step, b, c, rows].astype(F32)
                held[at] = total.astype(BF)
                return carry

            lax.fori_loop(0, side * side, add, 0)
            self.exchange(number, 1, self.second, order, lo, hi)

    def phase_second(self):
        held, second, side, place = self.grads_ref, self.second, self.side, self.place
        for number, (lo, hi, order) in enumerate(self.streams):
            rows = pl.ds(lo, hi - lo)
            self.arrived(number, 1)

            def add(c, carry, rows=rows, order=order):
                at = self.place_of(order, (place.at[order[0]], place.at[order[1]], c)) + (rows,)
                at = (place.core,) + at
                total = held[at].astype(F32)
                for step in range(side - 1):
                    total += second[step, c, rows].astype(F32)
                held[at] = total.astype(BF)
                return carry

            lax.fori_loop(0, side, add, 0)
            self.exchange(number, 2, self.third, order, lo, hi)

    def finish(self):
        for number, (lo, hi, order) in enumerate(self.streams):
            rows = pl.ds(lo, hi - lo)
            self.arrived(number, 2)
            total = self.grads_ref[(self.place.core,) + self.place.at + (rows,)].astype(F32)
            for step in range(self.side - 1):
                total += self.third[step, rows].astype(F32)
            self.out_ref[rows] = total
        for group in self.swaps + self.sends:
            for copy in group:
                copy.wait_send()


def reduce_scratch(sides, rows, streams):
    n, side = len(streams), sides[0]
    return [
        pltpu.VMEM(sides + (rows, 128), BF),
        pltpu.VMEM((side - 1, side, side, rows, 128), BF),
        pltpu.VMEM((side - 1, side, rows, 128), BF),
        pltpu.VMEM((side - 1, rows, 128), BF),
        pltpu.SemaphoreType.DMA((5,)),
        pltpu.SemaphoreType.DMA((5,)),
        pltpu.SemaphoreType.DMA((n, 3, side - 1)),
        pltpu.SemaphoreType.DMA((n, 3, side - 1)),
    ]


def pack_rows(pieces, rows):
    have = sum(piece.shape[0] for piece in pieces)
    if have < rows:
        pieces = pieces + [jnp.zeros((rows - have, 128), pieces[0].dtype)]
    return jnp.concatenate(pieces, 0)


def thin(block, count):
    return [block[:, 128 * t : 128 * t + 128] for t in range(count)]


def down_tail(tail):
    pieces = [tail[8 * b : 8 * b + 8] for b in range(6)]
    return jnp.concatenate(pieces + [jnp.zeros((8, 32), tail.dtype)], 1)


def open_tail(part):
    return jnp.concatenate([part[:, 16 * b : 16 * b + 16] for b in range(6)], 0)


def pack_weights(wq, wk, wv, wo, wg, wu, wd, gains, early_ref, late_ref):
    f = lambda ref: ref[...].astype(F32)
    out = f(wo)
    small = jnp.concatenate([f(wq), f(wk), f(wv), out[:, 128:]], 1)
    gain = jnp.concatenate([f(ref) for ref in gains], 0)
    gain = jnp.concatenate([gain, jnp.zeros((2, 128 - gain.shape[1]), F32)], 1)
    early_ref[...] = pack_rows(thin(small, 2) + [gain], EARLY).astype(BF)
    down = f(wd)
    late_ref[0:DOWN_AT] = pack_rows(thin(f(wg), 3) + thin(f(wu), 3), DOWN_AT).astype(BF)
    late_ref[DOWN_AT:TAIL_AT] = down[:, :128].astype(BF)
    tail = pack_rows([down_tail(down[:, 128:]), out[:, :128]], LATE - TAIL_AT)
    late_ref[TAIL_AT:LATE] = tail.astype(BF)


def unpack_early(slots, wqkv, tails):
    def block(x, carry):
        smalls = []
        for ctx in range(4):
            zh, core = ctx // 2, ctx % 2
            small = []
            for i in range(8):
                small.append(slots[core, x, i % 4, zh * 2 + i // 4].astype(F32))
            stack = lambda t: jnp.concatenate([b[18 * t : 18 * t + 18] for b in small], 0)
            smalls.append(jnp.concatenate([stack(t) for t in range(2)], 1))
        cut = lambda lo, hi: [part[:, lo:hi] for part in smalls]
        rows = pl.ds(pl.multiple_of(144 * x, 16), 144)
        whole = jnp.concatenate(cut(0, 144) + cut(144, 192) + cut(192, 240), 1)
        wqkv[rows, :] = whole.astype(BF)
        tails[rows, :] = jnp.concatenate(cut(240, 256), 1)
        return carry

    lax.fori_loop(0, 4, block, 0)


def unpack_gains(slots):
    pieces = []
    for x in range(4):
        for i in range(8):
            tile = slots[0, x, i % 4, i // 4, 32:48, :].astype(F32)
            pieces.append(tile[4:6, :18])
    return jnp.concatenate(pieces, 1)


def unpack_late(slots, tails, wo, wg, wu, wd):
    def block(x, carry):
        downs, outs = [[] for _ in range(8)], []
        rows = pl.ds(pl.multiple_of(144 * x, 16), 144)
        for ctx in range(4):
            zh, core = ctx // 2, ctx % 2
            gate, up, out = [], [], []
            for i in range(8):
                at = (core, x, i % 4, zh * 2 + i // 4)
                slot = slots[at].astype(F32)
                gate.append(slot[:UP_AT])
                up.append(slot[UP_AT : 2 * UP_AT])
                out.append(slot[OUT_AT : OUT_AT + 18])
                downs[i] += [slot[DOWN_AT:TAIL_AT], open_tail(slot[TAIL_AT:OUT_AT])]
            for t in range(3):
                lanes = slice(ctx * 384 + 128 * t, ctx * 384 + 128 * t + 128)
                stack = lambda blocks: jnp.concatenate(
                    [b[18 * t : 18 * t + 18] for b in blocks], 0
                )
                wg[rows, lanes] = stack(gate).astype(BF)
                wu[rows, lanes] = stack(up).astype(BF)
            outs += [jnp.concatenate(out, 0), tails[rows, 16 * ctx : 16 * ctx + 16]]
        wo[rows, :] = jnp.concatenate(outs, 1).astype(BF)
        for i in range(8):
            at = pl.ds(pl.multiple_of(384 * x + 48 * i, 16), 48)
            wd[at, :] = jnp.concatenate(downs[i], 1).astype(BF)
        return carry

    lax.fori_loop(0, 4, block, 0)


def pack_wide(gg, gu, zh, slots):
    def block(x, carry):
        rows = pl.ds(pl.multiple_of(144 * x, 16), 144)
        for core in range(2):
            lanes = slice(384 * core, 384 * core + 384)
            gate, up = gg[rows, lanes], gu[rows, lanes]
            for i in range(8):
                at = slice(18 * i, 18 * i + 18)
                slot = pack_rows(thin(gate[at], 3) + thin(up[at], 3), DOWN_AT).astype(BF)
                slots[core, x, i % 4, zh * 2 + i // 4, 0:DOWN_AT] = slot
        return carry

    lax.fori_loop(0, 4, block, 0)


def pack_down(gd, x, slots, tails):
    for ctx in range(4):
        zh, core = ctx // 2, ctx % 2
        for i in range(8):
            part = gd[48 * i : 48 * i + 48, 144 * ctx : 144 * ctx + 144]
            slots[core, x, i % 4, zh * 2 + i // 4, DOWN_AT:TAIL_AT] = part[:, :128].astype(BF)
            tails[x, i, ctx] = down_tail(part[:, 128:])


def pack_out(go, tails, slots):
    def block(x, carry):
        out = go[pl.ds(pl.multiple_of(144 * x, 16), 144), :]
        for ctx in range(4):
            zh, core = ctx // 2, ctx % 2
            main = out[:, 144 * ctx : 144 * ctx + 128]
            for i in range(8):
                pieces = [tails[x, i, ctx], main[18 * i : 18 * i + 18]]
                slot = pack_rows(pieces, LATE - TAIL_AT).astype(BF)
                slots[core, x, i % 4, zh * 2 + i // 4, TAIL_AT:LATE] = slot
        return carry

    lax.fori_loop(0, 4, block, 0)


def pack_early(gqkv, go, gains, out_ref):
    def block(x, carry):
        rows = pl.ds(pl.multiple_of(144 * x, 16), 144)
        whole = gqkv[rows, :]
        out = go[rows, :]
        for ctx in range(4):
            zh, core = ctx // 2, ctx % 2
            small = jnp.concatenate(
                [
                    whole[:, 144 * ctx : 144 * ctx + 144],
                    whole[:, D + 48 * ctx : D + 48 * ctx + 48],
                    whole[:, D + KV + 48 * ctx : D + KV + 48 * ctx + 48],
                    out[:, 144 * ctx + 128 : 144 * ctx + 144],
                ],
                1,
            )
            for i in range(8):
                pieces = thin(small[18 * i : 18 * i + 18], 2) + [gains[x, i]]
                slot = pack_rows(pieces, EARLY).astype(BF)
                out_ref[core, x, i % 4, zh * 2 + i // 4] = slot
        return carry

    lax.fori_loop(0, 4, block, 0)


def finish_kernel(early, late, out, dx, out_to, dx_to, ga, gm, gq, gk, gv, go, gg, gu, gd):
    def wide(slot, base, count):
        return jnp.concatenate(
            [slot[base + 18 * t : base + 18 * t + 18] for t in range(count)], 1
        )

    gg[...] = wide(late, 0, 3)
    gu[...] = wide(late, UP_AT, 3)
    gd[...] = jnp.concatenate([late[DOWN_AT:TAIL_AT], open_tail(late[TAIL_AT:OUT_AT])], 1)
    small = wide(early, 0, 2)
    gq[...] = small[:, :144]
    gk[...] = small[:, 144:192]
    gv[...] = small[:, 192:240]
    go[...] = jnp.concatenate([late[OUT_AT : OUT_AT + 18], small[:, 240:256]], 1)
    ga[...] = early[36:37, :18]
    gm[...] = early[37:38, :18]
    out_to[...] = out[...]
    dx_to[...] = dx[...]


def three_heads(ref, g, half, size):
    lanes = slice(half * size, half * size + size)
    base = g * GROUP * HEAD
    heads = [ref[base + HEAD * j : base + HEAD * j + HEAD, lanes] for j in range(GROUP)]
    return jnp.concatenate(heads, 1)


def turn(vectors, cosine, sine):
    first, second = vectors[: HEAD // 2], vectors[HEAD // 2 :]
    return jnp.concatenate([first * cosine - second * sine, second * cosine + first * sine], 0)


def columns_of(rows):
    full = jnp.concatenate([rows, jnp.zeros((2, 64), F32)], 1)
    turned = jnp.concatenate([full, jnp.zeros((126, 640), F32)], 0).T
    return turned[:D, 0:1], turned[:D, 1:2]


def rows_of(first, second):
    lane = lax.broadcasted_iota(jnp.int32, (D, 128), 1)
    full = jnp.where(lane == 0, first, jnp.where(lane == 1, second, 0.0))
    full = jnp.concatenate([full, jnp.zeros((64, 128), F32)], 0)
    return full.T[0:2, :D]


def causal(size):
    key = lax.broadcasted_iota(jnp.int32, (size, GROUP * size), 0)
    query = lax.broadcasted_iota(jnp.int32, (size, GROUP * size), 1) % size
    return key <= query


def mul(a, b, ca, cb):
    return lax.dot_general(a, b, (((ca,), (cb,)), ((), ())), preferred_element_type=F32)


class Context:
    def __init__(self, place, size):
        ctx = lax.axis_index("ctx")
        half, core = ctx // 2, ctx % 2
        self.size = size
        self.me = ctx
        self.sibling = half * 2 + 1 - core
        self.partner = (1 - half) * 2 + core
        self.corner = (1 - half) * 2 + 1 - core
        self.sibling_device = place.sibling()
        self.partner_device = place.peer(2, place.sides[2] // 2)

    def pairs(self, owner):
        late = jnp.where(owner > self.me, 1, 0)
        first, second = 1, late
        return (first, pl.ds(0, self.size)), (
            second,
            pl.ds(pl.multiple_of(late * self.size, self.size), self.size),
        )


def layer_kernel(sides, early_streams, late_gather, late_reduce, *refs):
    x_ref, dy_ref, wq, wk, wv, wo_ref, wg_ref, wu_ref, wd_ref = refs[:9]
    gain_a, gain_b, cos_ref, sin_ref = refs[9:13]
    out_ref, dx_ref, early_ref, total_ref = refs[13:17]
    scratch = refs[17:]
    early_slot, late_slot, early_slots, late_slots, kv_ref, kv_all = scratch[:6]
    queries, tops, totals, mixes, grads, lses, deltas, dqs = scratch[6:14]
    mixed_ref, normed_ref, wqkv, wo, wg, wu, wd, tails = scratch[14:22]
    middle, dmiddle, high, rising, falling, gate_grad, up_grad = scratch[22:29]
    out_grad, down_tails, acc, sent, passed, got, dqkv, gqkv, gain_rows = scratch[29:38]
    dy_rows = scratch[69]
    kv_sem, kv_send, kv_recv, back_send, back_recv = scratch[38:43]
    early_sems, late_sems = scratch[43:48], scratch[48:53]
    late_scratch, early_scratch = scratch[53:61], scratch[61:69]
    size = x_ref.shape[1] // 2
    place = Place(sides)
    ctx = Context(place, size)
    pack_weights(
        wq, wk, wv, wo_ref, wg_ref, wu_ref, wd_ref, (gain_a, gain_b), early_slot, late_slot
    )
    greet(place)
    early = Gather(place, early_streams, early_slot, early_slots, early_sems)
    gather = Gather(place, late_gather, late_slot, late_slots, late_sems)
    early.start()
    gather.start()

    def scale_of(values):
        return lax.rsqrt(jnp.mean(values * values, 0, keepdims=True) + 1e-05)

    inputs = x_ref[...].astype(F32)
    scale_one = scale_of(inputs)
    middle[...] = inputs * scale_one
    early.phase(1)
    gather.phase(1)
    early.phase(2)
    dy_rows[...] = dy_ref[...].astype(F32).T.astype(BF)
    for step in range(1, max(sides)):
        early.arrive(step)
    gather.phase(2)
    early.finish()
    unpack_early(early_slots, wqkv, tails)
    gain_one, gain_two = columns_of(unpack_gains(early_slots))
    normed_ref[...] = (middle[...] * gain_one).astype(BF)
    tables = [(cos_ref[b], sin_ref[b]) for b in (ctx.me, 7 - ctx.me)]
    pre = mul(wqkv[:, D:], normed_ref[...], 0, 0)
    for g in range(KV_HEADS):
        for half in range(2):
            lanes = slice(half * size, half * size + size)
            key = turn(pre[HEAD * g : HEAD * g + HEAD, lanes], *tables[half])
            both = jnp.concatenate([key, pre[KV + HEAD * g : KV + HEAD * g + HEAD, lanes]], 0)
            kv_ref[g, lanes, :] = both.T.astype(BF)
    far, near, corner = [], [], []
    for g in range(KV_HEADS):
        mine = kv_all.at[ctx.me, g]
        copy = remote(kv_ref.at[g], mine, kv_send.at[0, g], kv_recv.at[0, g], ctx.partner_device)
        copy.start()
        far.append(copy)
    for g in range(KV_HEADS):
        mine = kv_all.at[ctx.me, g]
        copy = remote(kv_ref.at[g], mine, kv_send.at[1, g], kv_recv.at[1, g], ctx.sibling_device)
        copy.start()
        near.append(copy)
    own = pltpu.make_async_copy(kv_ref, kv_all.at[ctx.me], kv_sem)
    own.start()
    for g in range(KV_HEADS):
        columns = slice(g * GROUP * HEAD, (g + 1) * GROUP * HEAD)
        pre = mul(wqkv[:, columns], normed_ref[...], 0, 0)
        for j in range(GROUP):
            for half in range(2):
                lanes = slice(half * size, half * size + size)
                turned = turn(pre[HEAD * j : HEAD * j + HEAD, lanes], *tables[half])
                turned = (turned * HEAD**-0.5).astype(BF)
                queries[g, half, :, size * j : size * j + size] = turned

    mask = causal(size)

    def scores_of(part):
        g, half, kv, masked = part[:4]
        scores = mul(kv[:, :HEAD], queries[g, half], 1, 0)
        return jnp.where(mask, scores, -1e30) if masked else scores

    def attend(parts):
        ahead = scores_of(parts[0])
        for n, (g, half, kv, masked, fresh) in enumerate(parts):
            scores = ahead
            if n + 1 < len(parts):
                ahead = scores_of(parts[n + 1])
            top = jnp.max(scores, 0, keepdims=True)
            if not fresh:
                before = tops[g, half]
                top = jnp.maximum(before, top)
            probs = jnp.exp(scores - top)
            total = jnp.sum(probs, 0, keepdims=True)
            mixed = mul(kv[:, HEAD:], probs.astype(BF), 0, 0)
            if not fresh:
                fade = jnp.exp(before - top)
                total += totals[g, half] * fade
                mixed += mixes[g, half] * fade
            tops[g, half], totals[g, half], mixes[g, half] = top, total, mixed

    def other(owner):
        parts = []
        for g in range(KV_HEADS):
            for half, rows in ctx.pairs(owner):
                parts.append((g, half, kv_all[owner, g, rows, :], False, False))
        attend(parts)

    parts = []
    for g in range(KV_HEADS):
        first, second = kv_ref[g, :size, :], kv_ref[g, size:, :]
        parts.append((g, 0, first, True, True))
        parts.append((g, 1, first, False, True))
        parts.append((g, 1, second, True, False))
    attend(parts)
    for copy in near:
        copy.wait_recv()
    other(ctx.sibling)
    for g in range(KV_HEADS):
        far[g].wait_recv()
        block = kv_all.at[ctx.partner, g]
        copy = remote(block, block, kv_send.at[2, g], kv_recv.at[2, g], ctx.sibling_device)
        copy.start()
        corner.append(copy)
    gather.arrive(1)
    other(ctx.partner)
    gather.arrive(2)
    for copy in corner:
        copy.wait_recv()
    own.wait()
    gather.arrive(3)
    other(ctx.corner)
    for g in range(KV_HEADS):
        for half in range(2):
            total = totals[g, half]
            mixed = (mixes[g, half] / total).astype(BF)
            lses[g, half] = tops[g, half] + jnp.log(total)
            lanes = slice(half * size, half * size + size)
            for j in range(GROUP):
                at = HEAD * (GROUP * g + j)
                mixed_ref[at : at + HEAD, lanes] = mixed[:, size * j : size * j + size]
    gather.finish()
    for copy in far + near + corner:
        copy.wait_send()

    unpack_late(late_slots, tails, wo, wg, wu, wd)
    middle[...] = x_ref[...].astype(F32) + mul(wo[...], mixed_ref[...], 0, 0)
    scale_two = scale_of(middle[...])
    normed_two = middle[...] * scale_two * gain_two
    high[...] = normed_two.astype(BF)
    low = normed_two.T.astype(BF)
    dy = dy_rows[...]
    rising[...] = jnp.zeros_like(rising)
    falling[...] = jnp.zeros_like(falling)

    reduce = Reduce(place, late_reduce, late_slots, total_ref, late_scratch)
    every = slice(None)

    def wide_swap(zh):
        two = pl.ds(pl.multiple_of(2 * zh, 2), 2)
        return reduce.swap(zh, (every, every, two, pl.ds(0, DOWN_AT)))

    def down_swap(x):
        two = pl.ds(pl.multiple_of(2 * x, 2), 2)
        return reduce.swap(2 + x, (two, every, every, pl.ds(DOWN_AT, TAIL_AT - DOWN_AT)))

    def chunk(c, carry):
        lanes = pl.ds(pl.multiple_of(2 * 384 * c, 256), 2 * 384)
        gate_w, up_w, down_w = wg[:, lanes], wu[:, lanes], wd[lanes, :]
        gate = mul(low, gate_w, 1, 0)
        upper = mul(low, up_w, 1, 0)
        dhid = mul(dy, down_w, 1, 1)
        sigma = jax.nn.sigmoid(gate)
        silu = gate * sigma
        hidden = (silu * upper).astype(BF)
        dgate = (dhid * upper * sigma * (1.0 + gate * (1.0 - sigma))).astype(BF)
        dup = (dhid * silu).astype(BF)
        rising[...] += mul(hidden, down_w, 1, 0)
        falling[...] += mul(dgate, gate_w, 1, 1) + mul(dup, up_w, 1, 1)
        gate_grad[...] = mul(high[...], dgate, 1, 0)
        up_grad[...] = mul(high[...], dup, 1, 0)
        pack_wide(gate_grad, up_grad, c, late_slots)
        wide_swap(c).start()
        down_grad = mul(hidden, dy, 0, 0)
        for k in range(2):
            pack_down(down_grad[384 * k : 384 * k + 384], 2 * c + k, late_slots, down_tails)
        down_swap(c).start()
        return carry

    lax.fori_loop(0, 2, chunk, 0)
    out_ref[...] = (middle[...] + rising[...].T).astype(BF)
    grad = falling[...].T
    gain_grad_two = jnp.sum(grad * middle[...] * scale_two, 1, keepdims=True)
    gained = grad * gain_two
    dmiddle[...] = (
        dy_ref[...].astype(F32)
        + scale_two * gained
        - middle[...] * scale_two**3 * jnp.mean(middle[...] * gained, 0, keepdims=True)
    )
    dattn = dmiddle[...].astype(BF)
    out_grad[...] = mul(mixed_ref[...], dattn, 1, 1)
    pack_out(out_grad, down_tails, late_slots)
    late_early = Reduce(place, early_streams, early_slots, early_ref, early_scratch)
    tail_swap = reduce.swap(4, (every, every, every, pl.ds(TAIL_AT, LATE - TAIL_AT)))
    tail_swap.start()
    wides, downs = [wide_swap(0), wide_swap(1)], [down_swap(0), down_swap(1)]
    reduce.swaps = [wides, downs, [tail_swap]]
    dmixed = mul(wo[...], dattn, 1, 0).astype(BF)
    for g in range(KV_HEADS):
        for half in range(2):
            grad = three_heads(dmixed, g, half, size)
            grads[g, half] = grad
            mixed = three_heads(mixed_ref, g, half, size)
            deltas[g, half] = jnp.sum(grad.astype(F32) * mixed.astype(F32), 0, keepdims=True)
    dqs[...] = jnp.zeros_like(dqs)

    def lead(part):
        g, half, kv, masked = part[:4]
        return scores_of(part), mul(kv[:, HEAD:], grads[g, half], 1, 0)

    def retrace(parts, give):
        ahead = lead(parts[0])
        for n, part in enumerate(parts):
            g, half, kv, masked = part
            scores, dprobs = ahead
            if n + 1 < len(parts):
                ahead = lead(parts[n + 1])
            probs = jnp.exp(scores - lses[g, half])
            dscores = (probs * (dprobs - deltas[g, half])).astype(BF)
            dvalue = mul(probs.astype(BF), grads[g, half], 1, 1)
            dkey = mul(dscores, queries[g, half], 1, 1)
            dqs[g, half] += mul(kv[:, :HEAD], dscores, 0, 0)
            give(n, g, jnp.concatenate([dkey, dvalue], 1))

    def back(owner, store):
        parts = []
        for g in range(KV_HEADS):
            for half, rows in ctx.pairs(owner):
                parts.append((g, half, kv_all[owner, g, rows, :], False))
        late = jnp.full((size, 128), owner, jnp.int32) > ctx.me
        kept = []

        def give(n, g, dkv):
            kept.append(dkv)
            if n % 2 == 1:
                store(g, kept[-2] + jnp.where(late, 0.0, dkv), jnp.where(late, dkv, 0.0))

        retrace(parts, give)

    def to_sibling(slot):
        def store(g, first, second):
            sent[slot, g, :size] = first.astype(BF)
            sent[slot, g, size:] = second.astype(BF)

        return store

    def to_acc(g, first, second):
        acc[g, :size] = first
        acc[g, size:] = second

    def send(slot):
        copies = []
        for g in range(KV_HEADS):
            copy = remote(
                sent.at[slot, g],
                got.at[slot, g],
                back_send.at[slot, g],
                back_recv.at[slot, g],
                ctx.sibling_device,
            )
            copy.start()
            copies.append(copy)
        return copies

    back(ctx.corner, to_sibling(0))
    copies = send(0)
    reduce.phase_pair()
    back(ctx.partner, to_acc)
    for copy in copies:
        copy.wait_recv()
    far = []
    for g in range(KV_HEADS):
        passed[g] = (acc[g] + got[0, g].astype(F32)).astype(BF)
        copy = remote(
            passed.at[g], got.at[2, g], back_send.at[2, g], back_recv.at[2, g], ctx.partner_device
        )
        copy.start()
        far.append(copy)
    back(ctx.sibling, to_sibling(1))
    near = send(1)
    parts, kept = [], []
    for g in range(KV_HEADS):
        first, second = kv_all[ctx.me, g, :size, :], kv_all[ctx.me, g, size:, :]
        parts += [(g, 0, first, True), (g, 1, first, False), (g, 1, second, True)]

    def keep(n, g, dkv):
        kept.append(dkv)
        if n % 3 == 2:
            to_acc(g, kept[-3] + kept[-2], dkv)

    retrace(parts, keep)
    for g in range(KV_HEADS):
        for half in range(2):
            lanes = slice(half * size, half * size + size)
            cosine, sine = tables[half]
            for j in range(GROUP):
                dquery = dqs[g, half, :, size * j : size * j + size] * HEAD**-0.5
                at = HEAD * (GROUP * g + j)
                dqkv[at : at + HEAD, lanes] = turn(dquery, cosine, -sine).astype(BF)
    for g in range(KV_HEADS):
        near[g].wait_recv()
        far[g].wait_recv()
        whole = (acc[g] + got[1, g].astype(F32) + got[2, g].astype(F32)).T
        at = D + HEAD * g
        for half in range(2):
            lanes = slice(half * size, half * size + size)
            cosine, sine = tables[half]
            dqkv[at : at + HEAD, lanes] = turn(whole[:HEAD, lanes], cosine, -sine).astype(BF)
        dqkv[at + KV : at + KV + HEAD, :] = whole[HEAD:].astype(BF)
    gqkv[...] = mul(normed_ref[...], dqkv[...], 1, 1)
    grad = mul(wqkv[...], dqkv[...], 1, 0)
    inputs = x_ref[...].astype(F32)
    scale_one = scale_of(inputs)
    gain_grad_one = jnp.sum(grad * inputs * scale_one, 1, keepdims=True)
    gain_grads = rows_of(gain_grad_one, gain_grad_two)
    for x in range(4):
        for i in range(8):
            at = 18 * (8 * x + i)
            gain_rows[x, i, :, 0:18] = gain_grads[:, at : at + 18]
    pack_early(gqkv, out_grad, gain_rows, early_slots)
    late_early.start()
    gained = grad * gain_one
    dx_ref[...] = (
        dmiddle[...]
        + scale_one * gained
        - inputs * scale_one**3 * jnp.mean(inputs * gained, 0, keepdims=True)
    )
    reduce.phase_first()
    late_early.phase_pair()
    reduce.phase_second()
    late_early.phase_first()
    late_early.phase_second()
    reduce.finish()
    late_early.finish()
    for copy in copies + far + near:
        copy.wait_send()


def layer(tokens, cotangent, weights, gains, sides):
    rows = tokens.shape[1]
    size = rows // 2
    vmem = pl.BlockSpec(memory_space=pltpu.VMEM)
    wide = GROUP * size
    kv = (KV_HEADS, rows, 2 * HEAD)
    heads = lambda height, kind: pltpu.VMEM((KV_HEADS, 2, height, wide), kind)
    dma = pltpu.SemaphoreType.DMA
    return pl.pallas_call(
        functools.partial(layer_kernel, sides, EARLY_STREAMS, LATE_GATHER, LATE_REDUCE),
        out_shape=[
            jax.ShapeDtypeStruct((D, rows), BF),
            jax.ShapeDtypeStruct((D, rows), F32),
            jax.ShapeDtypeStruct((EARLY, 128), F32),
            jax.ShapeDtypeStruct((LATE, 128), F32),
        ],
        in_specs=[vmem] * 13,
        out_specs=[vmem] * 4,
        scratch_shapes=[
            pltpu.VMEM((EARLY, 128), BF),
            pltpu.VMEM((LATE, 128), BF),
            pltpu.VMEM((2,) + sides + (EARLY, 128), BF),
            pltpu.VMEM((2,) + sides + (LATE, 128), BF),
            pltpu.VMEM(kv, BF),
            pltpu.VMEM((4,) + kv, BF),
            heads(HEAD, BF),
            heads(1, F32),
            heads(1, F32),
            heads(HEAD, F32),
            heads(HEAD, BF),
            heads(1, F32),
            heads(1, F32),
            heads(HEAD, F32),
            pltpu.VMEM((D, rows), BF),
            pltpu.VMEM((D, rows), BF),
            pltpu.VMEM((D, D + 2 * KV), BF),
            pltpu.VMEM((D, D), BF),
            pltpu.VMEM((D, FF), BF),
            pltpu.VMEM((D, FF), BF),
            pltpu.VMEM((FF, D), BF),
            pltpu.VMEM((D, 64), F32),
            pltpu.VMEM((D, rows), F32),
            pltpu.VMEM((D, rows), F32),
            pltpu.VMEM((D, rows), BF),
            pltpu.VMEM((rows, D), F32),
            pltpu.VMEM((rows, D), F32),
            pltpu.VMEM((D, FF // 2), F32),
            pltpu.VMEM((D, FF // 2), F32),
            pltpu.VMEM((D, D), F32),
            pltpu.VMEM((4, 8, 4, 8, 128), F32),
            pltpu.VMEM(kv, F32),
            pltpu.VMEM((2,) + kv, BF),
            pltpu.VMEM(kv, BF),
            pltpu.VMEM((3,) + kv, BF),
            pltpu.VMEM((D + 2 * KV, rows), BF),
            pltpu.VMEM((D, D + 2 * KV), F32),
            pltpu.VMEM((4, 8, 2, 128), F32),
            dma,
            dma((3, KV_HEADS)),
            dma((3, KV_HEADS)),
            dma((3, KV_HEADS)),
            dma((3, KV_HEADS)),
        ]
        + gather_sems(sides, EARLY_STREAMS)
        + gather_sems(sides, LATE_GATHER)
        + reduce_scratch(sides, LATE, LATE_REDUCE)
        + reduce_scratch(sides, EARLY, EARLY_STREAMS)
        + [pltpu.VMEM((rows, D), BF)],
        compiler_params=pltpu.CompilerParams(
            collective_id=0, has_side_effects=True, vmem_limit_bytes=VMEM_LIMIT
        ),
        name="decoder_layer",
    )(tokens, cotangent, *weights, *gains, *angles(size))


def angles(size):
    freq = 100000.0 ** (-np.arange(HEAD // 2) * 2.0 / HEAD)
    pos = np.arange(8 * size).reshape(8, 1, size)
    angle = pos * freq[None, :, None]
    return jnp.asarray(np.cos(angle), F32), jnp.asarray(np.sin(angle), F32)


def shards(
    tokens, cotangent, gain_attn, gain_mlp, w_query, w_key, w_value, w_out, w_gate, w_up, w_down
):
    sides = (4, 4, 4)
    result, grad_inputs, early_total, late_total = layer(
        tokens[0].T,
        cotangent[0].T,
        (w_query, w_key, w_value, w_out, w_gate, w_up, w_down),
        (gain_attn[None], gain_mlp[None]),
        sides,
    )
    shapes = [(1, 18), (1, 18), (18, 144), (18, 48), (18, 48), (18, 144), (18, 384), (18, 384)]
    out, dx, ga, gm, *grads = pl.pallas_call(
        finish_kernel,
        out_shape=[
            jax.ShapeDtypeStruct(result.shape, BF),
            jax.ShapeDtypeStruct(grad_inputs.shape, F32),
        ]
        + [jax.ShapeDtypeStruct(shape, F32) for shape in shapes + [(48, 144)]],
        name="finish",
    )(early_total, late_total, result, grad_inputs)
    return (out.T[None], dx.T[None], ga[0], gm[0], *grads)


def solution(mesh):
    both = P("dp", "ctx")
    block = P("dp", "ctx", None)
    return jax.shard_map(
        shards,
        mesh=mesh,
        in_specs=(block, block, P("dp"), P("dp")) + (both,) * 7,
        out_specs=(block, block, P("dp"), P("dp")) + (both,) * 7,
        check_vma=False,
    )
```

```python
import functools

import jax
import jax.numpy as jnp
import numpy as np
from jax import lax
from jax.experimental import pallas as pl
from jax.experimental.pallas import tpu as pltpu
from jax.sharding import PartitionSpec as P

D = 576
HEADS = 9
KV_HEADS = 3
HEAD = 64
GROUP = HEADS // KV_HEADS
FF = 1536
KV = KV_HEADS * HEAD
MESH = pl.DeviceIdType.MESH
BF = jnp.bfloat16
F32 = jnp.float32

EARLY = 48
LATE = 192
EARLY_STREAMS = ((0, 16, (0, 1, 2)), (16, 32, (1, 2, 0)), (32, 48, (2, 0, 1)))
LATE_GATHER = ((0, 80, (2, 1, 0)), (80, 160, (2, 0, 1)), (160, 192, (0, 1, 2)))
LATE_REDUCE = ((0, 80, (0, 1, 2)), (80, 160, (1, 0, 2)), (160, 192, (2, 0, 1)))
UP_AT, DOWN_AT, TAIL_AT, OUT_AT = 54, 112, 160, 168
VMEM_LIMIT = 60 * 1024 * 1024


class Place:
    def __init__(self, sides):
        self.sides = sides
        nx, ny, nz = sides
        self.low = nz // 2
        dp = lax.axis_index("dp")
        ctx = lax.axis_index("ctx")
        x = dp // (self.low * ny)
        y = dp % ny
        z = (ctx // 2) * self.low + (dp // ny) % self.low
        self.at = (x, y, z)
        self.core = ctx % 2

    def device(self, at, core):
        x, y, z = at
        dp = (x * self.low + z % self.low) * self.sides[1] + y
        return (dp, (z // self.low) * 2 + core)

    def shifted(self, axis, step):
        at = list(self.at)
        n = self.sides[axis]
        at[axis] = lax.rem(at[axis] + (step + n), n)
        return tuple(at)

    def peer(self, axis, step):
        return self.device(self.shifted(axis, step), self.core)

    def sibling(self):
        return self.device(self.at, 1 - self.core)


def greet(place):
    barrier = pltpu.get_barrier_semaphore()
    friends = [place.sibling()]
    for axis in range(3):
        for step in range(1, place.sides[axis]):
            friends.append(place.peer(axis, step))
    for friend in friends:
        pl.semaphore_signal(barrier, inc=1, device_id=friend, device_id_type=MESH)
    pl.semaphore_wait(barrier, len(friends))


def remote(src, dst, send_sem, recv_sem, device):
    return pltpu.make_async_remote_copy(
        src_ref=src,
        dst_ref=dst,
        send_sem=send_sem,
        recv_sem=recv_sem,
        device_id=device,
        device_id_type=MESH,
    )


class Gather:
    def __init__(self, place, streams, slot_ref, out_ref, sems):
        self.place, self.streams = place, streams
        self.slot_ref, self.out_ref = slot_ref, out_ref
        self.local_sem, self.send_sem, self.recv_sem, self.pair_send, self.pair_recv = sems
        self.sends = [[] for _ in streams]
        self.pairs = []

    def region(self, free, at, lo, hi):
        index = tuple(slice(None) if axis in free else at[axis] for axis in range(3))
        return self.out_ref.at[(self.place.core,) + index + (pl.ds(lo, hi - lo),)]

    def exchange(self, number, phase, src, free, axis, lo, hi):
        for step in range(1, self.place.sides[axis]):
            copy = remote(
                src,
                self.region(free, self.place.at, lo, hi),
                self.send_sem.at[number, phase, step - 1],
                self.recv_sem.at[number, phase, step - 1],
                self.place.peer(axis, step),
            )
            copy.start()
            self.sends[number].append(copy)

    def start(self):
        for number, (lo, hi, order) in enumerate(self.streams):
            src = self.slot_ref.at[pl.ds(lo, hi - lo)]
            self.exchange(number, 0, src, (), order[0], lo, hi)
        own = self.out_ref.at[(self.place.core,) + self.place.at]
        self.local = pltpu.make_async_copy(self.slot_ref, own, self.local_sem)
        self.local.start()

    def relay(self, number, step, at, lo, hi, order):
        plane = self.region(order[:2], at, lo, hi)
        copy = remote(
            plane,
            plane,
            self.pair_send.at[number, step],
            self.pair_recv.at[number, step],
            self.place.sibling(),
        )
        copy.start()
        self.pairs.append(copy)

    def phase(self, phase):
        if phase == 1:
            self.local.wait()
        for number, (lo, hi, order) in enumerate(self.streams):
            for copy in self.sends[number][-(self.place.sides[order[phase - 1]] - 1) :]:
                copy.wait_recv()
            free = order[:phase]
            src = self.region(free, self.place.at, lo, hi)
            self.exchange(number, phase, src, free, order[phase], lo, hi)
        if phase == 2:
            for number, (lo, hi, order) in enumerate(self.streams):
                self.relay(number, 0, self.place.at, lo, hi, order)

    def arrive(self, step):
        for number, (lo, hi, order) in enumerate(self.streams):
            axis = order[2]
            if step < self.place.sides[axis]:
                self.sends[number][step - self.place.sides[axis]].wait_recv()
                self.relay(number, step, self.place.shifted(axis, -step), lo, hi, order)

    def finish(self):
        for group in self.sends:
            for copy in group:
                copy.wait_send()
        for copy in self.pairs:
            copy.wait()


def gather_sems(sides, streams):
    n, side = len(streams), max(sides)
    return [
        pltpu.SemaphoreType.DMA,
        pltpu.SemaphoreType.DMA((n, 3, side - 1)),
        pltpu.SemaphoreType.DMA((n, 3, side - 1)),
        pltpu.SemaphoreType.DMA((n, side)),
        pltpu.SemaphoreType.DMA((n, side)),
    ]


class Reduce:
    def __init__(self, place, streams, grads_ref, out_ref, scratch):
        self.place, self.streams = place, streams
        self.grads_ref, self.out_ref = grads_ref, out_ref
        self.pair, self.first, self.second, self.third = scratch[:4]
        self.pair_send, self.pair_recv, self.send_sem, self.recv_sem = scratch[4:]
        self.side = place.sides[0]
        self.sends = [[] for _ in streams]

    def swap(self, index, at):
        return remote(
            self.grads_ref.at[(1 - self.place.core,) + at],
            self.pair.at[at],
            self.pair_send.at[index],
            self.pair_recv.at[index],
            self.place.sibling(),
        )

    def start(self):
        self.swaps = []
        for number, (lo, hi, order) in enumerate(self.streams):
            copy = self.swap(number, (slice(None),) * 3 + (pl.ds(lo, hi - lo),))
            copy.start()
            self.swaps.append([copy])

    def place_of(self, order, coords):
        index = [None, None, None]
        for axis, coord in zip(order, coords):
            index[axis] = coord
        return tuple(index)

    def exchange(self, number, phase, buffers, order, lo, hi):
        rows = pl.ds(lo, hi - lo)
        place, axis = self.place, order[phase]
        for step in range(1, self.side):
            fixed = [place.at[order[i]] for i in range(phase)]
            coords = fixed + [place.shifted(axis, step)[axis]] + [slice(None)] * (2 - phase)
            copy = remote(
                self.grads_ref.at[(place.core,) + self.place_of(order, coords) + (rows,)],
                buffers.at[(step - 1,) + (slice(None),) * (2 - phase) + (rows,)],
                self.send_sem.at[number, phase, step - 1],
                self.recv_sem.at[number, phase, step - 1],
                place.peer(axis, step),
            )
            copy.start()
            self.sends[number].append(copy)

    def arrived(self, number, phase):
        for copy in self.sends[number][phase * (self.side - 1) : (phase + 1) * (self.side - 1)]:
            copy.wait_recv()

    def phase_pair(self, numbers=(0, 1, 2)):
        held, pair, side, core = self.grads_ref, self.pair, self.side, self.place.core
        for number in numbers:
            lo, hi, order = self.streams[number]
            rows = pl.ds(lo, hi - lo)
            for copy in self.swaps[number]:
                copy.wait_recv()

            def add(i, carry, rows=rows):
                a, b = i // side, i % side
                for c in range(side):
                    at = (core, a, b, c, rows)
                    held[at] = (held[at].astype(F32) + pair[at[1:]].astype(F32)).astype(BF)
                return carry

            lax.fori_loop(0, side * side, add, 0)
            self.exchange(number, 0, self.first, order, lo, hi)

    def phase_first(self):
        held, first, side, place = self.grads_ref, self.first, self.side, self.place
        for number, (lo, hi, order) in enumerate(self.streams):
            rows = pl.ds(lo, hi - lo)
            self.arrived(number, 0)

            def add(i, carry, rows=rows, order=order):
                b, c = i // side, i % side
                axes = (order[0],) + tuple(sorted(order[1:]))
                at = self.place_of(axes, (place.at[order[0]], b, c)) + (rows,)
                at = (place.core,) + at
                total = held[at].astype(F32)
                for step in range(side - 1):
                    total += first[step, b, c, rows].astype(F32)
                held[at] = total.astype(BF)
                return carry

            lax.fori_loop(0, side * side, add, 0)
            self.exchange(number, 1, self.second, order, lo, hi)

    def phase_second(self):
        held, second, side, place = self.grads_ref, self.second, self.side, self.place
        for number, (lo, hi, order) in enumerate(self.streams):
            rows = pl.ds(lo, hi - lo)
            self.arrived(number, 1)

            def add(c, carry, rows=rows, order=order):
                at = self.place_of(order, (place.at[order[0]], place.at[order[1]], c)) + (rows,)
                at = (place.core,) + at
                total = held[at].astype(F32)
                for step in range(side - 1):
                    total += second[step, c, rows].astype(F32)
                held[at] = total.astype(BF)
                return carry

            lax.fori_loop(0, side, add, 0)
            self.exchange(number, 2, self.third, order, lo, hi)

    def finish(self):
        for number, (lo, hi, order) in enumerate(self.streams):
            rows = pl.ds(lo, hi - lo)
            self.arrived(number, 2)
            total = self.grads_ref[(self.place.core,) + self.place.at + (rows,)].astype(F32)
            for step in range(self.side - 1):
                total += self.third[step, rows].astype(F32)
            self.out_ref[rows] = total
        for group in self.swaps + self.sends:
            for copy in group:
                copy.wait_send()


def reduce_scratch(sides, rows, streams):
    n, side = len(streams), sides[0]
    return [
        pltpu.VMEM(sides + (rows, 128), BF),
        pltpu.VMEM((side - 1, side, side, rows, 128), BF),
        pltpu.VMEM((side - 1, side, rows, 128), BF),
        pltpu.VMEM((side - 1, rows, 128), BF),
        pltpu.SemaphoreType.DMA((5,)),
        pltpu.SemaphoreType.DMA((5,)),
        pltpu.SemaphoreType.DMA((n, 3, side - 1)),
        pltpu.SemaphoreType.DMA((n, 3, side - 1)),
    ]


def pack_rows(pieces, rows):
    have = sum(piece.shape[0] for piece in pieces)
    if have < rows:
        pieces = pieces + [jnp.zeros((rows - have, 128), pieces[0].dtype)]
    return jnp.concatenate(pieces, 0)


def thin(block, count):
    return [block[:, 128 * t : 128 * t + 128] for t in range(count)]


def down_tail(tail):
    pieces = [tail[8 * b : 8 * b + 8] for b in range(6)]
    return jnp.concatenate(pieces + [jnp.zeros((8, 32), tail.dtype)], 1)


def open_tail(part):
    return jnp.concatenate([part[:, 16 * b : 16 * b + 16] for b in range(6)], 0)


def pack_weights(wq, wk, wv, wo, wg, wu, wd, gains, early_ref, late_ref):
    f = lambda ref: ref[...].astype(F32)
    out = f(wo)
    small = jnp.concatenate([f(wq), f(wk), f(wv), out[:, 128:]], 1)
    gain = jnp.concatenate([f(ref) for ref in gains], 0)
    gain = jnp.concatenate([gain, jnp.zeros((2, 128 - gain.shape[1]), F32)], 1)
    early_ref[...] = pack_rows(thin(small, 2) + [gain], EARLY).astype(BF)
    down = f(wd)
    late_ref[0:DOWN_AT] = pack_rows(thin(f(wg), 3) + thin(f(wu), 3), DOWN_AT).astype(BF)
    late_ref[DOWN_AT:TAIL_AT] = down[:, :128].astype(BF)
    tail = pack_rows([down_tail(down[:, 128:]), out[:, :128]], LATE - TAIL_AT)
    late_ref[TAIL_AT:LATE] = tail.astype(BF)


def unpack_early(slots, wqkv, tails):
    def block(x, carry):
        smalls = []
        for ctx in range(4):
            zh, core = ctx // 2, ctx % 2
            small = []
            for i in range(8):
                small.append(slots[core, x, i % 4, zh * 2 + i // 4].astype(F32))
            stack = lambda t: jnp.concatenate([b[18 * t : 18 * t + 18] for b in small], 0)
            smalls.append(jnp.concatenate([stack(t) for t in range(2)], 1))
        cut = lambda lo, hi: [part[:, lo:hi] for part in smalls]
        rows = pl.ds(pl.multiple_of(144 * x, 16), 144)
        whole = jnp.concatenate(cut(0, 144) + cut(144, 192) + cut(192, 240), 1)
        wqkv[rows, :] = whole.astype(BF)
        tails[rows, :] = jnp.concatenate(cut(240, 256), 1)
        return carry

    lax.fori_loop(0, 4, block, 0)


def unpack_gains(slots):
    pieces = []
    for x in range(4):
        for i in range(8):
            tile = slots[0, x, i % 4, i // 4, 32:48, :].astype(F32)
            pieces.append(tile[4:6, :18])
    return jnp.concatenate(pieces, 1)


def unpack_late(slots, tails, wo, wg, wu, wd):
    def block(x, carry):
        downs, outs = [[] for _ in range(8)], []
        rows = pl.ds(pl.multiple_of(144 * x, 16), 144)
        for ctx in range(4):
            zh, core = ctx // 2, ctx % 2
            gate, up, out = [], [], []
            for i in range(8):
                at = (core, x, i % 4, zh * 2 + i // 4)
                slot = slots[at].astype(F32)
                gate.append(slot[:UP_AT])
                up.append(slot[UP_AT : 2 * UP_AT])
                out.append(slot[OUT_AT : OUT_AT + 18])
                downs[i] += [slot[DOWN_AT:TAIL_AT], open_tail(slot[TAIL_AT:OUT_AT])]
            for t in range(3):
                lanes = slice(ctx * 384 + 128 * t, ctx * 384 + 128 * t + 128)
                stack = lambda blocks: jnp.concatenate(
                    [b[18 * t : 18 * t + 18] for b in blocks], 0
                )
                wg[rows, lanes] = stack(gate).astype(BF)
                wu[rows, lanes] = stack(up).astype(BF)
            outs += [jnp.concatenate(out, 0), tails[rows, 16 * ctx : 16 * ctx + 16]]
        wo[rows, :] = jnp.concatenate(outs, 1).astype(BF)
        for i in range(8):
            at = pl.ds(pl.multiple_of(384 * x + 48 * i, 16), 48)
            wd[at, :] = jnp.concatenate(downs[i], 1).astype(BF)
        return carry

    lax.fori_loop(0, 4, block, 0)


def pack_wide(gg, gu, zh, slots):
    def block(x, carry):
        rows = pl.ds(pl.multiple_of(144 * x, 16), 144)
        for core in range(2):
            lanes = slice(384 * core, 384 * core + 384)
            gate, up = gg[rows, lanes], gu[rows, lanes]
            for i in range(8):
                at = slice(18 * i, 18 * i + 18)
                slot = pack_rows(thin(gate[at], 3) + thin(up[at], 3), DOWN_AT).astype(BF)
                slots[core, x, i % 4, zh * 2 + i // 4, 0:DOWN_AT] = slot
        return carry

    lax.fori_loop(0, 4, block, 0)


def pack_down(gd, x, slots, tails):
    for ctx in range(4):
        zh, core = ctx // 2, ctx % 2
        for i in range(8):
            part = gd[48 * i : 48 * i + 48, 144 * ctx : 144 * ctx + 144]
            slots[core, x, i % 4, zh * 2 + i // 4, DOWN_AT:TAIL_AT] = part[:, :128].astype(BF)
            tails[x, i, ctx] = down_tail(part[:, 128:])


def pack_out(go, tails, slots):
    def block(x, carry):
        out = go[pl.ds(pl.multiple_of(144 * x, 16), 144), :]
        for ctx in range(4):
            zh, core = ctx // 2, ctx % 2
            main = out[:, 144 * ctx : 144 * ctx + 128]
            for i in range(8):
                pieces = [tails[x, i, ctx], main[18 * i : 18 * i + 18]]
                slot = pack_rows(pieces, LATE - TAIL_AT).astype(BF)
                slots[core, x, i % 4, zh * 2 + i // 4, TAIL_AT:LATE] = slot
        return carry

    lax.fori_loop(0, 4, block, 0)


def pack_early(gqkv, go, gains, out_ref):
    def block(x, carry):
        rows = pl.ds(pl.multiple_of(144 * x, 16), 144)
        whole = gqkv[rows, :]
        out = go[rows, :]
        for ctx in range(4):
            zh, core = ctx // 2, ctx % 2
            small = jnp.concatenate(
                [
                    whole[:, 144 * ctx : 144 * ctx + 144],
                    whole[:, D + 48 * ctx : D + 48 * ctx + 48],
                    whole[:, D + KV + 48 * ctx : D + KV + 48 * ctx + 48],
                    out[:, 144 * ctx + 128 : 144 * ctx + 144],
                ],
                1,
            )
            for i in range(8):
                pieces = thin(small[18 * i : 18 * i + 18], 2) + [gains[x, i]]
                slot = pack_rows(pieces, EARLY).astype(BF)
                out_ref[core, x, i % 4, zh * 2 + i // 4] = slot
        return carry

    lax.fori_loop(0, 4, block, 0)


def finish_kernel(early, late, out, dx, out_to, dx_to, ga, gm, gq, gk, gv, go, gg, gu, gd):
    def wide(slot, base, count):
        return jnp.concatenate(
            [slot[base + 18 * t : base + 18 * t + 18] for t in range(count)], 1
        )

    gg[...] = wide(late, 0, 3)
    gu[...] = wide(late, UP_AT, 3)
    gd[...] = jnp.concatenate([late[DOWN_AT:TAIL_AT], open_tail(late[TAIL_AT:OUT_AT])], 1)
    small = wide(early, 0, 2)
    gq[...] = small[:, :144]
    gk[...] = small[:, 144:192]
    gv[...] = small[:, 192:240]
    go[...] = jnp.concatenate([late[OUT_AT : OUT_AT + 18], small[:, 240:256]], 1)
    ga[...] = early[36:37, :18]
    gm[...] = early[37:38, :18]
    out_to[...] = out[...]
    dx_to[...] = dx[...]


def three_heads(ref, g, half, size):
    lanes = slice(half * size, half * size + size)
    base = g * GROUP * HEAD
    heads = [ref[base + HEAD * j : base + HEAD * j + HEAD, lanes] for j in range(GROUP)]
    return jnp.concatenate(heads, 1)


def turn(vectors, cosine, sine):
    first, second = vectors[: HEAD // 2], vectors[HEAD // 2 :]
    return jnp.concatenate([first * cosine - second * sine, second * cosine + first * sine], 0)


def columns_of(rows):
    full = jnp.concatenate([rows, jnp.zeros((2, 64), F32)], 1)
    turned = jnp.concatenate([full, jnp.zeros((126, 640), F32)], 0).T
    return turned[:D, 0:1], turned[:D, 1:2]


def rows_of(first, second):
    lane = lax.broadcasted_iota(jnp.int32, (D, 128), 1)
    full = jnp.where(lane == 0, first, jnp.where(lane == 1, second, 0.0))
    full = jnp.concatenate([full, jnp.zeros((64, 128), F32)], 0)
    return full.T[0:2, :D]


def causal(size):
    key = lax.broadcasted_iota(jnp.int32, (size, GROUP * size), 0)
    query = lax.broadcasted_iota(jnp.int32, (size, GROUP * size), 1) % size
    return key <= query


def mul(a, b, ca, cb):
    return lax.dot_general(a, b, (((ca,), (cb,)), ((), ())), preferred_element_type=F32)


class Context:
    def __init__(self, place, size):
        ctx = lax.axis_index("ctx")
        half, core = ctx // 2, ctx % 2
        self.size = size
        self.me = ctx
        self.sibling = half * 2 + 1 - core
        self.partner = (1 - half) * 2 + core
        self.corner = (1 - half) * 2 + 1 - core
        self.sibling_device = place.sibling()
        self.partner_device = place.peer(2, place.sides[2] // 2)

    def pairs(self, owner):
        late = jnp.where(owner > self.me, 1, 0)
        first, second = 1, late
        return (first, pl.ds(0, self.size)), (
            second,
            pl.ds(pl.multiple_of(late * self.size, self.size), self.size),
        )


def layer_kernel(sides, early_streams, late_gather, late_reduce, *refs):
    x_ref, dy_ref, wq, wk, wv, wo_ref, wg_ref, wu_ref, wd_ref = refs[:9]
    gain_a, gain_b, cos_ref, sin_ref = refs[9:13]
    out_ref, dx_ref, early_ref, total_ref = refs[13:17]
    scratch = refs[17:]
    early_slot, late_slot, early_slots, late_slots, kv_ref, kv_all = scratch[:6]
    queries, tops, totals, mixes, grads, lses, deltas, dqs = scratch[6:14]
    mixed_ref, normed_ref, wqkv, wo, wg, wu, wd, tails = scratch[14:22]
    middle, dmiddle, high, rising, falling, gate_grad, up_grad = scratch[22:29]
    out_grad, down_tails, acc, sent, passed, got, dqkv, gqkv, gain_rows = scratch[29:38]
    dy_rows = scratch[69]
    kv_sem, kv_send, kv_recv, back_send, back_recv = scratch[38:43]
    early_sems, late_sems = scratch[43:48], scratch[48:53]
    late_scratch, early_scratch = scratch[53:61], scratch[61:69]
    size = x_ref.shape[1] // 2
    place = Place(sides)
    ctx = Context(place, size)
    pack_weights(
        wq, wk, wv, wo_ref, wg_ref, wu_ref, wd_ref, (gain_a, gain_b), early_slot, late_slot
    )
    greet(place)
    early = Gather(place, early_streams, early_slot, early_slots, early_sems)
    gather = Gather(place, late_gather, late_slot, late_slots, late_sems)
    early.start()
    gather.start()

    def scale_of(values):
        return lax.rsqrt(jnp.mean(values * values, 0, keepdims=True) + 1e-05)

    inputs = x_ref[...].astype(F32)
    scale_one = scale_of(inputs)
    middle[...] = inputs * scale_one
    early.phase(1)
    gather.phase(1)
    early.phase(2)
    dy_rows[...] = dy_ref[...].astype(F32).T.astype(BF)
    for step in range(1, max(sides)):
        early.arrive(step)
    gather.phase(2)
    early.finish()
    unpack_early(early_slots, wqkv, tails)
    gain_one, gain_two = columns_of(unpack_gains(early_slots))
    normed_ref[...] = (middle[...] * gain_one).astype(BF)
    tables = [(cos_ref[b], sin_ref[b]) for b in (ctx.me, 7 - ctx.me)]
    pre = mul(wqkv[:, D:], normed_ref[...], 0, 0)
    for g in range(KV_HEADS):
        for half in range(2):
            lanes = slice(half * size, half * size + size)
            key = turn(pre[HEAD * g : HEAD * g + HEAD, lanes], *tables[half])
            both = jnp.concatenate([key, pre[KV + HEAD * g : KV + HEAD * g + HEAD, lanes]], 0)
            kv_ref[g, lanes, :] = both.T.astype(BF)
    far, near, corner = [], [], []
    for g in range(KV_HEADS):
        mine = kv_all.at[ctx.me, g]
        copy = remote(kv_ref.at[g], mine, kv_send.at[0, g], kv_recv.at[0, g], ctx.partner_device)
        copy.start()
        far.append(copy)
    for g in range(KV_HEADS):
        mine = kv_all.at[ctx.me, g]
        copy = remote(kv_ref.at[g], mine, kv_send.at[1, g], kv_recv.at[1, g], ctx.sibling_device)
        copy.start()
        near.append(copy)
    own = pltpu.make_async_copy(kv_ref, kv_all.at[ctx.me], kv_sem)
    own.start()
    for g in range(KV_HEADS):
        columns = slice(g * GROUP * HEAD, (g + 1) * GROUP * HEAD)
        pre = mul(wqkv[:, columns], normed_ref[...], 0, 0)
        for j in range(GROUP):
            for half in range(2):
                lanes = slice(half * size, half * size + size)
                turned = turn(pre[HEAD * j : HEAD * j + HEAD, lanes], *tables[half])
                turned = (turned * HEAD**-0.5).astype(BF)
                queries[g, half, :, size * j : size * j + size] = turned

    mask = causal(size)

    def scores_of(part):
        g, half, kv, masked = part[:4]
        scores = mul(kv[:, :HEAD], queries[g, half], 1, 0)
        return jnp.where(mask, scores, -1e30) if masked else scores

    def attend(parts):
        ahead = scores_of(parts[0])
        for n, (g, half, kv, masked, fresh) in enumerate(parts):
            scores = ahead
            if n + 1 < len(parts):
                ahead = scores_of(parts[n + 1])
            top = jnp.max(scores, 0, keepdims=True)
            if not fresh:
                before = tops[g, half]
                top = jnp.maximum(before, top)
            probs = jnp.exp(scores - top)
            total = jnp.sum(probs, 0, keepdims=True)
            mixed = mul(kv[:, HEAD:], probs.astype(BF), 0, 0)
            if not fresh:
                fade = jnp.exp(before - top)
                total += totals[g, half] * fade
                mixed += mixes[g, half] * fade
            tops[g, half], totals[g, half], mixes[g, half] = top, total, mixed

    def other(owner):
        parts = []
        for g in range(KV_HEADS):
            for half, rows in ctx.pairs(owner):
                parts.append((g, half, kv_all[owner, g, rows, :], False, False))
        attend(parts)

    parts = []
    for g in range(KV_HEADS):
        first, second = kv_ref[g, :size, :], kv_ref[g, size:, :]
        parts.append((g, 0, first, True, True))
        parts.append((g, 1, first, False, True))
        parts.append((g, 1, second, True, False))
    attend(parts)
    for copy in near:
        copy.wait_recv()
    other(ctx.sibling)
    for g in range(KV_HEADS):
        far[g].wait_recv()
        block = kv_all.at[ctx.partner, g]
        copy = remote(block, block, kv_send.at[2, g], kv_recv.at[2, g], ctx.sibling_device)
        copy.start()
        corner.append(copy)
    gather.arrive(1)
    other(ctx.partner)
    gather.arrive(2)
    for copy in corner:
        copy.wait_recv()
    own.wait()
    gather.arrive(3)
    other(ctx.corner)
    for g in range(KV_HEADS):
        for half in range(2):
            total = totals[g, half]
            mixed = (mixes[g, half] / total).astype(BF)
            lses[g, half] = tops[g, half] + jnp.log(total)
            lanes = slice(half * size, half * size + size)
            for j in range(GROUP):
                at = HEAD * (GROUP * g + j)
                mixed_ref[at : at + HEAD, lanes] = mixed[:, size * j : size * j + size]
    gather.finish()
    for copy in far + near + corner:
        copy.wait_send()

    unpack_late(late_slots, tails, wo, wg, wu, wd)
    middle[...] = x_ref[...].astype(F32) + mul(wo[...], mixed_ref[...], 0, 0)
    scale_two = scale_of(middle[...])
    normed_two = middle[...] * scale_two * gain_two
    high[...] = normed_two.astype(BF)
    low = normed_two.T.astype(BF)
    dy = dy_rows[...]
    rising[...] = jnp.zeros_like(rising)
    falling[...] = jnp.zeros_like(falling)

    reduce = Reduce(place, late_reduce, late_slots, total_ref, late_scratch)
    every = slice(None)

    def wide_swap(zh):
        two = pl.ds(pl.multiple_of(2 * zh, 2), 2)
        return reduce.swap(zh, (every, every, two, pl.ds(0, DOWN_AT)))

    def down_swap(x):
        two = pl.ds(pl.multiple_of(2 * x, 2), 2)
        return reduce.swap(2 + x, (two, every, every, pl.ds(DOWN_AT, TAIL_AT - DOWN_AT)))

    def chunk(c, carry):
        lanes = pl.ds(pl.multiple_of(2 * 384 * c, 256), 2 * 384)
        gate_w, up_w, down_w = wg[:, lanes], wu[:, lanes], wd[lanes, :]
        gate = mul(low, gate_w, 1, 0)
        upper = mul(low, up_w, 1, 0)
        dhid = mul(dy, down_w, 1, 1)
        sigma = jax.nn.sigmoid(gate)
        silu = gate * sigma
        hidden = (silu * upper).astype(BF)
        dgate = (dhid * upper * sigma * (1.0 + gate * (1.0 - sigma))).astype(BF)
        dup = (dhid * silu).astype(BF)
        rising[...] += mul(hidden, down_w, 1, 0)
        falling[...] += mul(dgate, gate_w, 1, 1) + mul(dup, up_w, 1, 1)
        gate_grad[...] = mul(high[...], dgate, 1, 0)
        up_grad[...] = mul(high[...], dup, 1, 0)
        pack_wide(gate_grad, up_grad, c, late_slots)
        wide_swap(c).start()
        down_grad = mul(hidden, dy, 0, 0)
        for k in range(2):
            pack_down(down_grad[384 * k : 384 * k + 384], 2 * c + k, late_slots, down_tails)
        down_swap(c).start()
        return carry

    lax.fori_loop(0, 2, chunk, 0)
    out_ref[...] = (middle[...] + rising[...].T).astype(BF)
    grad = falling[...].T
    gain_grad_two = jnp.sum(grad * middle[...] * scale_two, 1, keepdims=True)
    gained = grad * gain_two
    dmiddle[...] = (
        dy_ref[...].astype(F32)
        + scale_two * gained
        - middle[...] * scale_two**3 * jnp.mean(middle[...] * gained, 0, keepdims=True)
    )
    dattn = dmiddle[...].astype(BF)
    out_grad[...] = mul(mixed_ref[...], dattn, 1, 1)
    pack_out(out_grad, down_tails, late_slots)
    late_early = Reduce(place, early_streams, early_slots, early_ref, early_scratch)
    tail_swap = reduce.swap(4, (every, every, every, pl.ds(TAIL_AT, LATE - TAIL_AT)))
    tail_swap.start()
    wides, downs = [wide_swap(0), wide_swap(1)], [down_swap(0), down_swap(1)]
    reduce.swaps = [wides, downs, [tail_swap]]
    dmixed = mul(wo[...], dattn, 1, 0).astype(BF)
    for g in range(KV_HEADS):
        for half in range(2):
            grad = three_heads(dmixed, g, half, size)
            grads[g, half] = grad
            mixed = three_heads(mixed_ref, g, half, size)
            deltas[g, half] = jnp.sum(grad.astype(F32) * mixed.astype(F32), 0, keepdims=True)
    dqs[...] = jnp.zeros_like(dqs)

    def lead(part):
        g, half, kv, masked = part[:4]
        return scores_of(part), mul(kv[:, HEAD:], grads[g, half], 1, 0)

    def retrace(parts, give):
        ahead = lead(parts[0])
        for n, part in enumerate(parts):
            g, half, kv, masked = part
            scores, dprobs = ahead
            if n + 1 < len(parts):
                ahead = lead(parts[n + 1])
            probs = jnp.exp(scores - lses[g, half])
            dscores = (probs * (dprobs - deltas[g, half])).astype(BF)
            dvalue = mul(probs.astype(BF), grads[g, half], 1, 1)
            dkey = mul(dscores, queries[g, half], 1, 1)
            dqs[g, half] += mul(kv[:, :HEAD], dscores, 0, 0)
            give(n, g, jnp.concatenate([dkey, dvalue], 1))

    def back(owner, store):
        parts = []
        for g in range(KV_HEADS):
            for half, rows in ctx.pairs(owner):
                parts.append((g, half, kv_all[owner, g, rows, :], False))
        late = jnp.full((size, 128), owner, jnp.int32) > ctx.me
        kept = []

        def give(n, g, dkv):
            kept.append(dkv)
            if n % 2 == 1:
                store(g, kept[-2] + jnp.where(late, 0.0, dkv), jnp.where(late, dkv, 0.0))

        retrace(parts, give)

    def to_sibling(slot):
        def store(g, first, second):
            sent[slot, g, :size] = first.astype(BF)
            sent[slot, g, size:] = second.astype(BF)

        return store

    def to_acc(g, first, second):
        acc[g, :size] = first
        acc[g, size:] = second

    def send(slot):
        copies = []
        for g in range(KV_HEADS):
            copy = remote(
                sent.at[slot, g],
                got.at[slot, g],
                back_send.at[slot, g],
                back_recv.at[slot, g],
                ctx.sibling_device,
            )
            copy.start()
            copies.append(copy)
        return copies

    reduce.phase_pair((0, 1))
    back(ctx.corner, to_sibling(0))
    copies = send(0)
    reduce.phase_pair((2,))
    back(ctx.partner, to_acc)
    for copy in copies:
        copy.wait_recv()
    far = []
    for g in range(KV_HEADS):
        passed[g] = (acc[g] + got[0, g].astype(F32)).astype(BF)
        copy = remote(
            passed.at[g], got.at[2, g], back_send.at[2, g], back_recv.at[2, g], ctx.partner_device
        )
        copy.start()
        far.append(copy)
    back(ctx.sibling, to_sibling(1))
    near = send(1)
    parts, kept = [], []
    for g in range(KV_HEADS):
        first, second = kv_all[ctx.me, g, :size, :], kv_all[ctx.me, g, size:, :]
        parts += [(g, 0, first, True), (g, 1, first, False), (g, 1, second, True)]

    def keep(n, g, dkv):
        kept.append(dkv)
        if n % 3 == 2:
            to_acc(g, kept[-3] + kept[-2], dkv)

    retrace(parts, keep)
    for g in range(KV_HEADS):
        for half in range(2):
            lanes = slice(half * size, half * size + size)
            cosine, sine = tables[half]
            for j in range(GROUP):
                dquery = dqs[g, half, :, size * j : size * j + size] * HEAD**-0.5
                at = HEAD * (GROUP * g + j)
                dqkv[at : at + HEAD, lanes] = turn(dquery, cosine, -sine).astype(BF)
    for g in range(KV_HEADS):
        near[g].wait_recv()
        far[g].wait_recv()
        whole = (acc[g] + got[1, g].astype(F32) + got[2, g].astype(F32)).T
        at = D + HEAD * g
        for half in range(2):
            lanes = slice(half * size, half * size + size)
            cosine, sine = tables[half]
            dqkv[at : at + HEAD, lanes] = turn(whole[:HEAD, lanes], cosine, -sine).astype(BF)
        dqkv[at + KV : at + KV + HEAD, :] = whole[HEAD:].astype(BF)
    gqkv[...] = mul(normed_ref[...], dqkv[...], 1, 1)
    grad = mul(wqkv[...], dqkv[...], 1, 0)
    inputs = x_ref[...].astype(F32)
    scale_one = scale_of(inputs)
    gain_grad_one = jnp.sum(grad * inputs * scale_one, 1, keepdims=True)
    gain_grads = rows_of(gain_grad_one, gain_grad_two)
    for x in range(4):
        for i in range(8):
            at = 18 * (8 * x + i)
            gain_rows[x, i, :, 0:18] = gain_grads[:, at : at + 18]
    pack_early(gqkv, out_grad, gain_rows, early_slots)
    late_early.start()
    gained = grad * gain_one
    dx_ref[...] = (
        dmiddle[...]
        + scale_one * gained
        - inputs * scale_one**3 * jnp.mean(inputs * gained, 0, keepdims=True)
    )
    reduce.phase_first()
    late_early.phase_pair()
    reduce.phase_second()
    late_early.phase_first()
    late_early.phase_second()
    reduce.finish()
    late_early.finish()
    for copy in copies + far + near:
        copy.wait_send()


def layer(tokens, cotangent, weights, gains, sides):
    rows = tokens.shape[1]
    size = rows // 2
    vmem = pl.BlockSpec(memory_space=pltpu.VMEM)
    wide = GROUP * size
    kv = (KV_HEADS, rows, 2 * HEAD)
    heads = lambda height, kind: pltpu.VMEM((KV_HEADS, 2, height, wide), kind)
    dma = pltpu.SemaphoreType.DMA
    return pl.pallas_call(
        functools.partial(layer_kernel, sides, EARLY_STREAMS, LATE_GATHER, LATE_REDUCE),
        out_shape=[
            jax.ShapeDtypeStruct((D, rows), BF),
            jax.ShapeDtypeStruct((D, rows), F32),
            jax.ShapeDtypeStruct((EARLY, 128), F32),
            jax.ShapeDtypeStruct((LATE, 128), F32),
        ],
        in_specs=[vmem] * 13,
        out_specs=[vmem] * 4,
        scratch_shapes=[
            pltpu.VMEM((EARLY, 128), BF),
            pltpu.VMEM((LATE, 128), BF),
            pltpu.VMEM((2,) + sides + (EARLY, 128), BF),
            pltpu.VMEM((2,) + sides + (LATE, 128), BF),
            pltpu.VMEM(kv, BF),
            pltpu.VMEM((4,) + kv, BF),
            heads(HEAD, BF),
            heads(1, F32),
            heads(1, F32),
            heads(HEAD, F32),
            heads(HEAD, BF),
            heads(1, F32),
            heads(1, F32),
            heads(HEAD, F32),
            pltpu.VMEM((D, rows), BF),
            pltpu.VMEM((D, rows), BF),
            pltpu.VMEM((D, D + 2 * KV), BF),
            pltpu.VMEM((D, D), BF),
            pltpu.VMEM((D, FF), BF),
            pltpu.VMEM((D, FF), BF),
            pltpu.VMEM((FF, D), BF),
            pltpu.VMEM((D, 64), F32),
            pltpu.VMEM((D, rows), F32),
            pltpu.VMEM((D, rows), F32),
            pltpu.VMEM((D, rows), BF),
            pltpu.VMEM((rows, D), F32),
            pltpu.VMEM((rows, D), F32),
            pltpu.VMEM((D, FF // 2), F32),
            pltpu.VMEM((D, FF // 2), F32),
            pltpu.VMEM((D, D), F32),
            pltpu.VMEM((4, 8, 4, 8, 128), F32),
            pltpu.VMEM(kv, F32),
            pltpu.VMEM((2,) + kv, BF),
            pltpu.VMEM(kv, BF),
            pltpu.VMEM((3,) + kv, BF),
            pltpu.VMEM((D + 2 * KV, rows), BF),
            pltpu.VMEM((D, D + 2 * KV), F32),
            pltpu.VMEM((4, 8, 2, 128), F32),
            dma,
            dma((3, KV_HEADS)),
            dma((3, KV_HEADS)),
            dma((3, KV_HEADS)),
            dma((3, KV_HEADS)),
        ]
        + gather_sems(sides, EARLY_STREAMS)
        + gather_sems(sides, LATE_GATHER)
        + reduce_scratch(sides, LATE, LATE_REDUCE)
        + reduce_scratch(sides, EARLY, EARLY_STREAMS)
        + [pltpu.VMEM((rows, D), BF)],
        compiler_params=pltpu.CompilerParams(
            collective_id=0, has_side_effects=True, vmem_limit_bytes=VMEM_LIMIT
        ),
        name="decoder_layer",
    )(tokens, cotangent, *weights, *gains, *angles(size))


def angles(size):
    freq = 100000.0 ** (-np.arange(HEAD // 2) * 2.0 / HEAD)
    pos = np.arange(8 * size).reshape(8, 1, size)
    angle = pos * freq[None, :, None]
    return jnp.asarray(np.cos(angle), F32), jnp.asarray(np.sin(angle), F32)


def shards(
    tokens, cotangent, gain_attn, gain_mlp, w_query, w_key, w_value, w_out, w_gate, w_up, w_down
):
    sides = (4, 4, 4)
    result, grad_inputs, early_total, late_total = layer(
        tokens[0].T,
        cotangent[0].T,
        (w_query, w_key, w_value, w_out, w_gate, w_up, w_down),
        (gain_attn[None], gain_mlp[None]),
        sides,
    )
    shapes = [(1, 18), (1, 18), (18, 144), (18, 48), (18, 48), (18, 144), (18, 384), (18, 384)]
    out, dx, ga, gm, *grads = pl.pallas_call(
        finish_kernel,
        out_shape=[
            jax.ShapeDtypeStruct(result.shape, BF),
            jax.ShapeDtypeStruct(grad_inputs.shape, F32),
        ]
        + [jax.ShapeDtypeStruct(shape, F32) for shape in shapes + [(48, 144)]],
        name="finish",
    )(early_total, late_total, result, grad_inputs)
    return (out.T[None], dx.T[None], ga[0], gm[0], *grads)


def solution(mesh):
    both = P("dp", "ctx")
    block = P("dp", "ctx", None)
    return jax.shard_map(
        shards,
        mesh=mesh,
        in_specs=(block, block, P("dp"), P("dp")) + (both,) * 7,
        out_specs=(block, block, P("dp"), P("dp")) + (both,) * 7,
        check_vma=False,
    )
```
